32 devices in a mesh: dom: 4 (over y, x), rel: 8 (over z, core).
Axes of the slice: x: 2, y: 2, z: 4, core: 2. Of those that a mesh axis runs over, the one named last changes fastest.
Arguments:
- entity: float32 [4096, 512], P(('dom', 'rel')), may hold values from -1.8 to 1.8
- entity_acc: float32 [4096, 512], P(('dom', 'rel')), may hold values from 0.01 to 1
- relation: float32 [1024, 512], P('rel'), may hold values from -1 to 1, as said below
- relation_acc: float32 [1024, 512], P('rel'), may hold values from 0.01 to 1
- send_rows: int32 [32, 8, 16], P(('dom', 'rel')), may hold values from 0 to 127, as said below
- trip_head: int32 [8192], P(('dom', 'rel')), may hold values from 0 to 127
- trip_rel: int32 [8192], P(('dom', 'rel')), may hold values from 0 to 127
- trip_tail: int32 [8192], P(('dom', 'rel')), may hold values from 0 to 127
- neg_part: int32 [1], replicated, may hold values from 0 to 3
- neg_rows: int32 [8, 32], replicated, may hold values from 0 to 127
Outputs:
- new_entity: float32 [4096, 512], P(('dom', 'rel'))
- new_entity_acc: float32 [4096, 512], P(('dom', 'rel'))
- new_relation: float32 [1024, 512], P('rel')
- new_relation_acc: float32 [1024, 512], P('rel')
The draws below stay inside these ranges and needn't reach their ends.
Inputs may be any that keep to these rules, and one draw needn't show every extreme that they name: `send_rows`: within one owner's list for one receiver the 16 rows are distinct. `relation`: every component has magnitude 0.1 or more.
All inputs are finite; a program needn't handle non-finite values.
Results may differ from the reference program's by a relative error of at most 0.0003.
Values sent between devices are 32-bit elements; how exact they have to be, the bound alone decides.
No kernel may reach another device: no remote copies, remote signals or barrier semaphores. Data moves between devices by JAX's collectives and lax.ppermute only.
A program may use at most 64 MiB of HBM per device.

```python
import math
import jax
import jax.numpy as jnp
from jax import lax

RANK = 128
ENT_DEV = 128
REL_DEV = 128
TRIP_DEV = 256
SLOTS = 16
NEG_SLOT = 32
TOUCHED = 128
ENTS = 4096
RELS = 1024
TRIPLES = 8192
N_DOM = 4
N_REL = 8


def draw_relation(key, part):
    key_sign, key_size = jax.random.split(key)
    shape = (REL_DEV * N_REL, 4 * RANK)
    signs = jnp.where(jax.random.bernoulli(key_sign, 0.5, shape), 1.0, -1.0).astype(jnp.float32)
    magnitude = jax.random.uniform(key_size, shape, jnp.float32, 0.25, 1.0)
    return (signs * magnitude).astype(jnp.float32)


def draw_send_rows(key, part):
    shape = (N_DOM * N_REL, N_REL, ENT_DEV)
    scores = jax.random.randint(key, shape, 0, 2 ** 20) * ENT_DEV + lax.broadcasted_iota(jnp.int32, shape, 2)
    order = jnp.argsort(scores, axis=-1, stable=True)
    return order[:, :, :SLOTS].astype(jnp.int32)


def touch_ends(result, key, least, high):
    longest = result.shape.index(max(result.shape))
    spots = []
    for shift in (0, 1):
        where = [jax.random.randint(jax.random.fold_in(key, axis), (), 0, length) for axis, length in enumerate(result.shape)]
        where[longest] = (where[longest] + shift) % result.shape[longest]
        spots.append(tuple(where))
    return result.at[spots[0]].set(least).at[spots[1]].set(high)


def block_scale(key, extent, pieces, smallest, top_value):
    gain, own = 1.0, jax.random.fold_in(key, 6)
    for dim, parts in pieces:
        heights = jnp.exp(jax.random.uniform(jax.random.fold_in(own, dim), (parts,), jnp.float32, smallest / len(pieces), top_value / len(pieces)))
        gain = gain * jnp.repeat(heights, extent[dim] // parts).reshape([-1 if axis == dim else 1 for axis in range(len(extent))])
    return gain


def scatter_about(rng, dims, width, limit, pieces=(), kind=jnp.bfloat16):
    entries = width * jax.random.normal(rng, dims, jnp.float32)
    if pieces:
        entries = entries * block_scale(rng, dims, pieces, -0.22, 0.18)
    return jnp.clip(entries, -limit, limit).astype(kind)


def setup_inputs(seed: int = 0) -> dict:
    arg_keys = jax.random.split(jax.random.key(seed), 11)
    entity = scatter_about(arg_keys[0], (ENTS, 4 * RANK), 0.3, 1.8, ((0, 32),), jnp.float32)
    entity_acc = jnp.clip(jnp.exp(math.log(1.0) - 4.6051702 * jax.random.uniform(arg_keys[1], (ENTS, 4 * RANK), jnp.float32) ** block_scale(arg_keys[1], (ENTS, 4 * RANK), ((0, 32),), -0.2, 0.2)), 0.01, 1.0)
    relation = draw_relation(jax.random.fold_in(arg_keys[10], 71), 0)
    relation_acc = jnp.clip(jnp.exp(math.log(1.0) - 4.6051702 * jax.random.uniform(arg_keys[3], (RELS, 4 * RANK), jnp.float32) ** block_scale(arg_keys[3], (RELS, 4 * RANK), ((0, 8),), -0.2, 0.2)), 0.01, 1.0)
    send_rows = draw_send_rows(jax.random.fold_in(arg_keys[10], 71), 0)
    trip_head = touch_ends(jax.random.randint(arg_keys[5], (TRIPLES,), 0, TOUCHED), jax.random.fold_in(arg_keys[5], 1), 0, TOUCHED - 1).astype(jnp.int32)
    trip_rel = touch_ends(jax.random.randint(arg_keys[6], (TRIPLES,), 0, REL_DEV), jax.random.fold_in(arg_keys[6], 1), 0, REL_DEV - 1).astype(jnp.int32)
    trip_tail = touch_ends(jax.random.randint(arg_keys[7], (TRIPLES,), 0, TOUCHED), jax.random.fold_in(arg_keys[7], 1), 0, TOUCHED - 1).astype(jnp.int32)
    neg_part = jax.random.randint(arg_keys[8], (1,), 0, N_DOM).astype(jnp.int32)
    neg_rows = touch_ends(jax.random.randint(arg_keys[9], (N_REL, NEG_SLOT), 0, ENT_DEV), jax.random.fold_in(arg_keys[9], 1), 0, ENT_DEV - 1).astype(jnp.int32)
    return dict(entity=entity, entity_acc=entity_acc, relation=relation, relation_acc=relation_acc, send_rows=send_rows, trip_head=trip_head, trip_rel=trip_rel, trip_tail=trip_tail, neg_part=neg_part, neg_rows=neg_rows)


step_size = 0.05

def hamilton(left, right):
    left_a, left_b, left_c, left_d = jnp.split(left, 4, axis=-1)
    right_a, right_b, right_c, right_d = jnp.split(right, 4, axis=-1)
    out_a = left_a * right_a - left_b * right_b - left_c * right_c - left_d * right_d
    out_b = left_a * right_b + left_b * right_a + left_c * right_d - left_d * right_c
    out_c = left_a * right_c - left_b * right_d + left_c * right_a + left_d * right_b
    out_d = left_a * right_d + left_b * right_c - left_c * right_b + left_d * right_a
    return jnp.concatenate([out_a, out_b, out_c, out_d], axis=-1)

def unit_rel(relation):
    comp_a, comp_b, comp_c, comp_d = jnp.split(relation, 4, axis=-1)
    magnitude = jnp.sqrt(comp_a * comp_a + comp_b * comp_b + comp_c * comp_c + comp_d * comp_d)
    return relation / jnp.concatenate([magnitude, magnitude, magnitude, magnitude], axis=-1)

def local_loss(touched, relation, negatives, heads, rels, tails):
    unit_rows = unit_rel(relation)
    one_hot = (rels[:, None] == jnp.arange(relation.shape[0])[None, :]).astype(unit_rows.dtype)
    rotation = jnp.dot(one_hot, unit_rows, precision=lax.Precision.HIGHEST)
    query = hamilton(touched[heads], rotation)
    positive = lax.optimization_barrier(jnp.sum(query * touched[tails], axis=-1))
    scores = jnp.einsum('ik,jk->ij', query, negatives, precision=lax.Precision.HIGHEST)
    return jnp.sum(jax.nn.softplus(-positive)) + jnp.sum(jax.nn.softplus(scores)) / negatives.shape[0]

def adagrad(values, history, gradient):
    history_new = history + gradient * gradient
    return (values - step_size * gradient / jnp.sqrt(history_new), history_new)

def reference(entity, entity_acc, relation, relation_acc, send_rows, trip_head, trip_rel, trip_tail, neg_part, neg_rows):
    row_width = entity.shape[1]
    blocks = entity.reshape(N_DOM, N_REL, ENT_DEV, row_width)
    send_lists = send_rows.reshape(N_DOM, N_REL, N_REL, SLOTS)
    rel_blocks = relation.reshape(N_REL, REL_DEV, row_width)
    heads_all = trip_head.reshape(N_DOM * N_REL, TRIP_DEV)
    rels_all = trip_rel.reshape(N_DOM * N_REL, TRIP_DEV)
    tails_all = trip_tail.reshape(N_DOM * N_REL, TRIP_DEV)
    neg_root = neg_part[0]
    sources = jnp.arange(N_REL)[:, None]
    negatives = blocks[neg_root][sources, neg_rows].reshape(NEG_SLOT * N_REL, row_width)

    def device_step(carry, device):
        ent_grad, rel_grad, neg_grad = carry
        dom_here = device // N_REL
        rel_here = device % N_REL
        wanted = send_lists[dom_here][:, rel_here, :]
        touched = blocks[dom_here][sources, wanted].reshape(N_REL * SLOTS, row_width)
        rel_local = rel_blocks[rel_here]
        heads = heads_all[device]
        rels = rels_all[device]
        tails = tails_all[device]

        def scored(touched_in, relation_in, negatives_in):
            return local_loss(touched_in, relation_in, negatives_in, heads, rels, tails)
        loss_value, pullback = jax.vjp(scored, touched, rel_local, negatives)
        grad_rows, grad_rel, grad_neg = pullback(jnp.ones_like(loss_value))
        ent_grad = ent_grad.at[dom_here, sources, wanted].add(grad_rows.reshape(N_REL, SLOTS, row_width))
        rel_grad = rel_grad.at[rel_here].add(grad_rel)
        neg_grad = neg_grad + grad_neg
        return ((ent_grad, rel_grad, neg_grad), None)
    start = (jnp.zeros_like(blocks), jnp.zeros_like(rel_blocks), jnp.zeros_like(negatives))
    (ent_grad, rel_grad, neg_grad), _ = lax.scan(device_step, start, jnp.arange(N_DOM * N_REL))
    ent_grad = ent_grad.at[neg_root, sources, neg_rows].add(neg_grad.reshape(N_REL, NEG_SLOT, row_width))
    new_entity, new_entity_acc = adagrad(entity, entity_acc, ent_grad.reshape(-1, row_width))
    new_relation, new_relation_acc = adagrad(relation, relation_acc, rel_grad.reshape(-1, row_width))
    return (new_entity, new_entity_acc, new_relation, new_relation_acc)
```

```python
import jax
import jax.numpy as jnp
from jax import lax
from jax.sharding import PartitionSpec as P

step_size = 0.05
HIGHEST = lax.Precision.HIGHEST


def exchange(block, axis, size, step):
    return lax.ppermute(block, axis, [(i, i ^ step) for i in range(size)])


def dot(left, right, dims):
    return lax.dot_general(
        left, right, (dims, ((), ())), precision=HIGHEST, preferred_element_type=jnp.float32
    )


def one_hot(index, size):
    return (index[:, None] == jnp.arange(size)[None, :]).astype(jnp.float32)


def hamilton(left, right):
    la, lb, lc, ld = jnp.split(left, 4, axis=-1)
    ra, rb, rc, rd = jnp.split(right, 4, axis=-1)
    out_a = la * ra - lb * rb - lc * rc - ld * rd
    out_b = la * rb + lb * ra + lc * rd - ld * rc
    out_c = la * rc - lb * rd + lc * ra + ld * rb
    out_d = la * rd + lb * rc - lc * rb + ld * ra
    return jnp.concatenate([out_a, out_b, out_c, out_d], axis=-1)


def conjugate(rows):
    quarter = rows.shape[-1] // 4
    return jnp.concatenate([rows[:, :quarter], -rows[:, quarter:]], axis=-1)


def four(block):
    return jnp.concatenate([block] * 4, axis=-1)


def fold(rows):
    a, b, c, d = jnp.split(rows, 4, axis=-1)
    return a + b + c + d


def adagrad(values, history, gradient):
    history_new = history + gradient * gradient
    return (values - step_size * gradient / jnp.sqrt(history_new), history_new)


def shards(
    entity,
    entity_acc,
    relation,
    relation_acc,
    send_rows,
    trip_head,
    trip_rel,
    trip_tail,
    neg_part,
    neg_rows,
    *,
    n_dom,
    n_rel,
):
    ents, width = entity.shape
    rels = relation.shape[0]
    slots = send_rows.shape[2]
    n_chip = n_rel // 2
    dom_here = lax.axis_index("dom")
    rel_here = lax.axis_index("rel")
    neg_root = neg_part[0]

    lists = send_rows[0][jnp.arange(n_rel) ^ rel_here].reshape(n_chip, 2, slots)
    own_rows = neg_rows[rel_here]
    outgoing = entity[lists]
    own_negs = entity[own_rows]

    spread = [own_negs] + [exchange(own_negs, "dom", n_dom, s) for s in range(1, n_dom)]
    picked = lax.dynamic_index_in_dim(jnp.stack(spread), dom_here ^ neg_root, 0, keepdims=False)

    from_core = exchange(outgoing[:, 1], "rel", n_rel, 1)
    parcels = jnp.stack([outgoing[:, 0], from_core], axis=1)
    touched = [parcels[0]] + [exchange(parcels[s], "rel", n_rel, 2 * s) for s in range(1, n_chip)]
    touched = jnp.stack(touched).reshape(-1, width)

    half = [picked] + [exchange(picked, "rel", n_rel, 2 * s) for s in range(1, n_chip)]
    half = jnp.concatenate(half, axis=0)

    ra, rb, rc, rd = jnp.split(relation, 4, axis=-1)
    inverse = four(lax.rsqrt(ra * ra + rb * rb + rc * rc + rd * rd))
    unit = relation * inverse
    pick_rel = one_hot(trip_rel, rels)
    pick_head = one_hot(((trip_head // slots) ^ rel_here) * slots + trip_head % slots, n_rel * slots)
    pick_tail = one_hot(((trip_tail // slots) ^ rel_here) * slots + trip_tail % slots, n_rel * slots)
    rotation = dot(pick_rel, unit, ((1,), (0,)))
    head = dot(pick_head, touched, ((1,), (0,)))
    tail = dot(pick_tail, touched, ((1,), (0,)))
    query = hamilton(head, rotation)
    pull = -jax.nn.sigmoid(-jnp.sum(query * tail, axis=-1, keepdims=True))
    queries = jnp.concatenate([query, exchange(query, "rel", n_rel, 1)], axis=0)

    push = jax.nn.sigmoid(dot(queries, half, ((1,), (1,)))) / (2 * half.shape[0])
    grad_half = dot(push, queries, ((0,), (0,)))
    grad_queries = dot(push, half, ((1,), (0,)))

    parts = grad_half.reshape(n_chip, -1, width)
    neg_share = parts[0]
    for s in range(1, n_chip):
        neg_share = neg_share + exchange(parts[s], "rel", n_rel, 2 * s)
    neg_total = neg_share
    for s in range(1, n_dom):
        neg_total = neg_total + exchange(neg_share, "dom", n_dom, s)

    trips = query.shape[0]
    grad_query = grad_queries[:trips] + exchange(grad_queries[trips:], "rel", n_rel, 1) + pull * tail
    grad_head = hamilton(grad_query, conjugate(rotation))
    grad_rot = hamilton(conjugate(head), grad_query)
    grad_touched = dot(pick_head, grad_head, ((0,), (0,))) + dot(
        pick_tail, pull * query, ((0,), (0,))
    )
    grad_unit = dot(pick_rel, grad_rot, ((0,), (0,)))
    rel_grad = inverse * (grad_unit - unit * four(fold(unit * grad_unit)))

    back = grad_touched.reshape(n_chip, 2, slots, width)
    back = jnp.stack([back[0]] + [exchange(back[s], "rel", n_rel, 2 * s) for s in range(1, n_chip)])
    returned = jnp.stack([back[:, 0], exchange(back[:, 1], "rel", n_rel, 1)], axis=1)

    bits = [1 << b for b in range((n_dom - 1).bit_length())]
    middle = rels // 2
    low, high = rel_grad[:middle], rel_grad[middle:]
    for up, down in zip(bits, bits[::-1]):
        low = low + exchange(low, "dom", n_dom, up)
        high = high + exchange(high, "dom", n_dom, down)
    rel_sum = jnp.concatenate([low, high], axis=0)

    is_owner = (dom_here == neg_root).astype(jnp.float32)
    ent_grad = dot(one_hot(lists.reshape(-1), ents), returned.reshape(-1, width), ((0,), (0,)))
    ent_grad = ent_grad + dot(one_hot(own_rows, ents), is_owner * neg_total, ((0,), (0,)))
    new_entity, new_entity_acc = adagrad(entity, entity_acc, ent_grad)
    new_relation, new_relation_acc = adagrad(relation, relation_acc, rel_sum)
    return (new_entity, new_entity_acc, new_relation, new_relation_acc)


def solution(mesh):
    def step(*arrays):
        return shards(*arrays, n_dom=mesh.shape["dom"], n_rel=mesh.shape["rel"])

    both = ("dom", "rel")
    in_specs = (
        P(both, None),
        P(both, None),
        P("rel", None),
        P("rel", None),
        P(both, None, None),
        P(both),
        P(both),
        P(both),
        P(),
        P(),
    )
    out_specs = (P(both, None), P(both, None), P("rel", None), P("rel", None))
    return jax.shard_map(step, mesh=mesh, in_specs=in_specs, out_specs=out_specs, check_vma=False)
```

```python
import functools

import jax
import jax.numpy as jnp
from jax import lax
from jax.experimental import pallas as pl
from jax.experimental.pallas import tpu as pltpu
from jax.sharding import PartitionSpec as P

step_size = 0.05
SMEM = pl.BlockSpec(memory_space=pltpu.SMEM)
VMEM = pl.BlockSpec(memory_space=pltpu.VMEM)
HBM = pl.BlockSpec(memory_space=pltpu.HBM)
ROWS = ((1,), (0,))
COLS = ((1,), (1,))
LEFT = ((0,), (0,))


def exchange(block, axis, size, step):
    return lax.ppermute(block, axis, [(i, i ^ step) for i in range(size)])


def call(body, outs, specs, args, flops=0, scratch=()):
    shapes = [jax.ShapeDtypeStruct(shape, jnp.float32) for shape in outs]
    moved = 4 * sum(int(a.size) for a in args) + 4 * sum(int(s.size) for s in shapes)
    return pl.pallas_call(
        body,
        out_shape=shapes,
        in_specs=specs,
        out_specs=[VMEM] * len(shapes),
        scratch_shapes=scratch,
        compiler_params=pltpu.CompilerParams(vmem_limit_bytes=40 * 1024 * 1024),
        cost_estimate=pl.CostEstimate(flops=flops, bytes_accessed=moved, transcendentals=0),
    )(*args)


def dot(left, right, dims):
    return lax.dot_general(left, right, (dims, ((), ())), preferred_element_type=jnp.float32)


def halves(rows):
    high = rows.astype(jnp.bfloat16)
    low = (rows - high.astype(jnp.float32)).astype(jnp.bfloat16)
    return high, low


def pick(index, size):
    spots = lax.broadcasted_iota(jnp.int32, (size, index.shape[1]), 0)
    return (spots == index).astype(jnp.float32)


def take(chosen, table):
    high, low = halves(table)
    chosen = chosen.astype(jnp.bfloat16)
    return dot(
        jnp.concatenate([chosen, chosen], axis=0), jnp.concatenate([high, low], axis=0), LEFT
    )


def put(chosen, rows):
    high, low = halves(rows)
    chosen = chosen.astype(jnp.bfloat16)
    return dot(chosen, high, ROWS) + dot(chosen, low, ROWS)


def quarters(rows):
    size = rows.shape[-1] // 4
    return [rows[:, i * size : (i + 1) * size] for i in range(4)]


def hamilton(left, right):
    la, lb, lc, ld = left
    ra, rb, rc, rd = right
    return [
        la * ra - lb * rb - lc * rc - ld * rd,
        la * rb + lb * ra + lc * rd - ld * rc,
        la * rc - lb * rd + lc * ra + ld * rb,
        la * rd + lb * rc - lc * rb + ld * ra,
    ]


def conjugate(parts):
    return [parts[0], -parts[1], -parts[2], -parts[3]]


def join(parts):
    return jnp.concatenate(parts, axis=-1)


def gather_kernel(send_ref, neg_ref, entity_ref, negs_ref, keep_ref, give_ref, rows, sends, picks, sems):
    copies = [
        pltpu.make_async_copy(source, target, sems.at[i])
        for i, (source, target) in enumerate(
            ((entity_ref, rows), (send_ref, sends), (neg_ref, picks))
        )
    ]
    for copy in copies:
        copy.start()
    for copy in copies:
        copy.wait()
    rel_here = lax.axis_index("rel")
    slots = send_ref.shape[2]

    def neg_row(i, carry):
        negs_ref[pl.ds(i, 1), :] = rows[pl.ds(picks[rel_here, i], 1), :]
        return carry

    lax.fori_loop(0, neg_ref.shape[1], neg_row, 0, unroll=8)

    def chip(s, carry):
        for core, out in ((0, keep_ref), (1, give_ref)):
            peer = (2 * s + core) ^ rel_here
            for t in range(slots):
                out[pl.ds(s * slots + t, 1), :] = rows[pl.ds(sends[0, peer, t], 1), :]
        return carry

    lax.fori_loop(0, send_ref.shape[1] // 2, chip, 0)


def unit_parts(rows):
    parts = quarters(rows)
    inverse = lax.rsqrt(sum(part * part for part in parts))
    return [part * inverse for part in parts], inverse


def rotation_kernel(rel_index_ref, relation_ref, rot_ref):
    unit, _ = unit_parts(relation_ref[...])
    chosen = pick(rel_index_ref[...].reshape(1, -1), relation_ref.shape[0])
    rot_ref[...] = take(chosen, join(unit))


def relative(index_ref, rel_here, slots):
    index = index_ref[...].reshape(1, -1)
    return ((index // slots) ^ rel_here) * slots + index % slots


def both_picks(head_ref, tail_ref, slots, size):
    rel_here = lax.axis_index("rel")
    heads = pick(relative(head_ref, rel_here, slots), size)
    tails = pick(relative(tail_ref, rel_here, slots), size)
    return jnp.concatenate([heads, tails], axis=1)


def scores_kernel(
    slots, n_chip, head_ref, tail_ref, rot_ref, *refs
):
    parcels, blocks = refs[:n_chip], refs[n_chip : 3 * n_chip]
    mine_ref, theirs_ref, query_ref, head_out, tail_out, pull_ref, push_ref = refs[3 * n_chip :]
    touched = jnp.concatenate([ref[...] for ref in parcels], axis=0)
    negs = jnp.concatenate([ref[...] for ref in blocks], axis=0)
    trips = head_ref.shape[0]
    rows = take(both_picks(head_ref, tail_ref, slots, touched.shape[0]), touched)
    head, tail = rows[:trips], rows[trips:]
    query = join(hamilton(quarters(head), quarters(rot_ref[...])))
    positive = jnp.sum(query * tail, axis=-1, keepdims=True)
    pull_ref[...] = jnp.broadcast_to(-jax.nn.sigmoid(-positive), pull_ref.shape)
    query_ref[...], head_out[...], tail_out[...] = query, head, tail
    q_high, q_low = halves(query)
    n_high, n_low = halves(negs)
    scores = dot(q_high, n_high, COLS) + dot(q_high, n_low, COLS) + dot(q_low, n_high, COLS)
    push = jax.nn.sigmoid(scores) * (1.0 / negs.shape[0])
    push_ref[...] = push
    p_high, p_low = halves(push)
    grad = dot(p_high, q_high, LEFT) + dot(p_low, q_high, LEFT) + dot(p_high, q_low, LEFT)
    middle = mine_ref.shape[0]
    mine_ref[...] = grad[:middle]
    theirs_ref[...] = grad[middle:]


def grad_kernel(slots, n_chip, head_ref, rel_index_ref, tail_ref, relation_ref, rot_ref, *refs):
    blocks = refs[: 2 * n_chip]
    query_ref, head_rows, tail_rows, pull_ref, push_ref = refs[2 * n_chip : 2 * n_chip + 5]
    low_ref, high_ref, touched_ref = refs[2 * n_chip + 5 :]
    negs = jnp.concatenate([ref[...] for ref in blocks], axis=0)
    p_high, p_low = halves(push_ref[...])
    n_high, n_low = halves(negs)
    pulled = dot(p_high, n_high, ROWS) + dot(p_low, n_high, ROWS) + dot(p_high, n_low, ROWS)
    pull = pull_ref[:, :1]
    grad_query = quarters(pulled + pull * tail_rows[...])
    grad_head = join(hamilton(grad_query, conjugate(quarters(rot_ref[...]))))
    grad_rot = join(hamilton(conjugate(quarters(head_rows[...])), grad_query))
    grad_tail = pull * query_ref[...]
    chosen = both_picks(head_ref, tail_ref, slots, touched_ref.shape[0])
    touched_ref[...] = put(chosen, jnp.concatenate([grad_head, grad_tail], axis=0))
    unit, inverse = unit_parts(relation_ref[...])
    chosen = pick(rel_index_ref[...].reshape(1, -1), relation_ref.shape[0])
    grad_unit = quarters(put(chosen, grad_rot))
    along = sum(u * g for u, g in zip(unit, grad_unit))
    rel_grad = join([inverse * (g - u * along) for u, g in zip(unit, grad_unit)])
    middle = low_ref.shape[0]
    low_ref[...] = rel_grad[:middle]
    high_ref[...] = rel_grad[middle:]


def select_kernel(part_ref, after_ref, *refs):
    *blocks, out_ref = refs
    source = lax.axis_index("dom") ^ part_ref[0]
    picked = blocks[0][...]
    for s, ref in enumerate(blocks):
        picked = jnp.where(source == s, ref[...], picked)
    out_ref[...] = picked


def parcel_kernel(slots, own_ref, keep_ref, came_ref, copy_ref, *parcels):
    copy_ref[...] = own_ref[...]
    for s, ref in enumerate(parcels):
        rows = pl.ds(s * slots, slots)
        ref[:slots] = keep_ref[rows]
        ref[slots:] = came_ref[rows]


def pack_kernel(slots, n_neg, mine, theirs, touched, low, high, low_ref, high_ref, *back):
    low_ref[...] = low[...]
    high_ref[...] = high[...]
    for s, ref in enumerate(back):
        block = pl.ds(s * n_neg, n_neg)
        ref[: 2 * slots] = touched[2 * s * slots : 2 * (s + 1) * slots]
        ref[2 * slots :] = mine[block] + theirs[block]


def unpack_kernel(slots, n_chip, *refs):
    back, (neg_ref, stay_ref, cross_ref) = refs[:n_chip], refs[-3:]
    neg_ref[...] = sum(ref[2 * slots :] for ref in back)
    for s, ref in enumerate(back):
        rows = pl.ds(s * slots, slots)
        stay_ref[rows] = ref[:slots]
        cross_ref[rows] = ref[slots : 2 * slots]


def adagrad(values, history, gradient):
    history_new = history + gradient * gradient
    return values - step_size * gradient * lax.rsqrt(history_new), history_new


def entity_kernel(part_ref, send_ref, neg_ref, entity_ref, acc_ref, stay_ref, cross_ref, *refs):
    negs, (out_ref, acc_out) = refs[:-2], refs[-2:]
    rel_here = lax.axis_index("rel")
    owner = (lax.axis_index("dom") == part_ref[0]).astype(jnp.float32)
    size = entity_ref.shape[0]
    slots = send_ref.shape[2]
    neg = sum(ref[...] for ref in negs) * owner
    chosen = [pick(neg_ref[pl.ds(rel_here, 1), :], size)]
    rows = [neg]
    for k, ref in ((0, stay_ref), (1, cross_ref)):
        for s in range(send_ref.shape[1] // 2):
            peer = (2 * s + k) ^ rel_here
            chosen.append(pick(send_ref[0, pl.ds(peer, 1), :], size))
            rows.append(ref[s * slots : (s + 1) * slots])
    grad = put(jnp.concatenate(chosen, axis=1), jnp.concatenate(rows, axis=0))
    out_ref[...], acc_out[...] = adagrad(entity_ref[...], acc_ref[...], grad)


def relation_kernel(low_a, low_b, high_a, high_b, relation_ref, acc_ref, out_ref, acc_out):
    grad = jnp.concatenate([low_a[...] + low_b[...], high_a[...] + high_b[...]], axis=0)
    out_ref[...], acc_out[...] = adagrad(relation_ref[...], acc_ref[...], grad)


def shards(
    entity,
    entity_acc,
    relation,
    relation_acc,
    send_rows,
    trip_head,
    trip_rel,
    trip_tail,
    neg_part,
    neg_rows,
    *,
    n_dom,
    n_rel,
):
    ents, width = entity.shape
    rels = relation.shape[0]
    trips = trip_head.shape[0]
    slots = send_rows.shape[2]
    n_neg = neg_rows.shape[1]
    n_chip = n_rel // 2

    own_negs, keep, give = call(
        gather_kernel,
        [(n_neg, width), (n_chip * slots, width), (n_chip * slots, width)],
        [HBM, HBM, HBM],
        (send_rows, neg_rows, entity),
        scratch=[
            pltpu.VMEM(entity.shape, jnp.float32),
            pltpu.SMEM(send_rows.shape, jnp.int32),
            pltpu.SMEM(neg_rows.shape, jnp.int32),
            pltpu.SemaphoreType.DMA((3,)),
        ],
    )
    came = exchange(give, "rel", n_rel, 1)
    near = exchange(own_negs, "dom", n_dom, 1)
    copied, *parcels = call(
        functools.partial(parcel_kernel, slots),
        [own_negs.shape] + [(2 * slots, width)] * n_chip,
        [VMEM] * 3,
        (own_negs, keep, came),
    )
    arrived = [parcels[0]] + [exchange(parcels[s], "rel", n_rel, 2 * s) for s in range(1, n_chip)]
    spread = [copied, near] + [exchange(copied, "dom", n_dom, s) for s in range(2, n_dom)]
    (rot,) = call(rotation_kernel, [(trips, width)], [VMEM] * 2, (trip_rel, relation))
    (picked,) = call(
        select_kernel,
        [own_negs.shape],
        [SMEM, VMEM] + [VMEM] * n_dom,
        (neg_part, rot, *spread),
    )
    negs = [picked] + [exchange(picked, "rel", n_rel, 2 * s) for s in range(1, n_chip)]
    others = [exchange(block, "rel", n_rel, 1) for block in negs]

    mine, theirs, *saved = call(
        functools.partial(scores_kernel, slots, n_chip),
        [(n_chip * n_neg, width)] * 2 + [(trips, width)] * 3 + [(trips, 128), (trips, n_rel * n_neg)],
        [VMEM] * (3 + 3 * n_chip),
        (trip_head, trip_tail, rot, *arrived, *negs, *others),
    )
    theirs = exchange(theirs, "rel", n_rel, 1)
    low, high, touched = call(
        functools.partial(grad_kernel, slots, n_chip),
        [(rels // 2, width)] * 2 + [(n_rel * slots, width)],
        [VMEM] * (10 + 2 * n_chip),
        (trip_head, trip_rel, trip_tail, relation, rot, *negs, *others, *saved),
    )

    low, high, *back = call(
        functools.partial(pack_kernel, slots, n_neg),
        [low.shape, high.shape] + [(2 * slots + n_neg, width)] * n_chip,
        [VMEM] * 5,
        (mine, theirs, touched, low, high),
    )
    back = [back[0]] + [exchange(back[s], "rel", n_rel, 2 * s) for s in range(1, n_chip)]
    bits = [1 << b for b in range((n_dom - 1).bit_length())]
    sums = [[low], [high]]
    first = []
    for up, down in zip(bits, bits[::-1]):
        sums = [[sum(pair)] for pair in sums]
        first = first or ([sums[0][0], sums[1][0]] if len(bits) > 1 and up != bits[0] else [])
        sums[0].append(exchange(sums[0][0], "dom", n_dom, up))
        sums[1].append(exchange(sums[1][0], "dom", n_dom, down))
    neg_share, stay, cross = call(
        functools.partial(unpack_kernel, slots, n_chip),
        [(n_neg, width)] + [(n_chip * slots, width)] * 2,
        [VMEM] * (n_chip + len(first)),
        (*back, *first),
    )
    neg_shares = [neg_share] + [exchange(neg_share, "dom", n_dom, s) for s in range(1, n_dom)]
    cross = exchange(cross, "rel", n_rel, 1)

    new_relation, new_relation_acc = call(
        relation_kernel,
        [relation.shape] * 2,
        [VMEM] * 6,
        (*sums[0], *sums[1], relation, relation_acc),
    )

    new_entity, new_entity_acc = call(
        entity_kernel,
        [entity.shape] * 2,
        [SMEM] + [VMEM] * (6 + n_dom),
        (neg_part, send_rows, neg_rows, entity, entity_acc, stay, cross, *neg_shares),
    )
    return (new_entity, new_entity_acc, new_relation, new_relation_acc)


def solution(mesh):
    def step(*arrays):
        return shards(*arrays, n_dom=mesh.shape["dom"], n_rel=mesh.shape["rel"])

    both = ("dom", "rel")
    in_specs = (
        P(both, None),
        P(both, None),
        P("rel", None),
        P("rel", None),
        P(both, None, None),
        P(both),
        P(both),
        P(both),
        P(),
        P(),
    )
    out_specs = (P(both, None), P(both, None), P("rel", None), P("rel", None))
    return jax.shard_map(step, mesh=mesh, in_specs=in_specs, out_specs=out_specs, check_vma=False)
```

```python
import functools

import jax
import jax.numpy as jnp
from jax import lax
from jax.experimental import pallas as pl
from jax.experimental.pallas import tpu as pltpu
from jax.sharding import PartitionSpec as P

step_size = 0.05
SMEM = pl.BlockSpec(memory_space=pltpu.SMEM)
VMEM = pl.BlockSpec(memory_space=pltpu.VMEM)
HBM = pl.BlockSpec(memory_space=pltpu.HBM)
ROWS = ((1,), (0,))
COLS = ((1,), (1,))
LEFT = ((0,), (0,))


def exchange(block, axis, size, step):
    return lax.ppermute(block, axis, [(i, i ^ step) for i in range(size)])


def call(body, outs, specs, args, flops=0, scratch=(), limit=40, out_space=None):
    shapes = [jax.ShapeDtypeStruct(shape, jnp.float32) for shape in outs]
    moved = 4 * sum(int(a.size) for a in args) + 4 * sum(int(s.size) for s in shapes)
    return pl.pallas_call(
        body,
        out_shape=shapes,
        in_specs=specs,
        out_specs=[out_space or VMEM] * len(shapes),
        scratch_shapes=scratch,
        compiler_params=pltpu.CompilerParams(vmem_limit_bytes=limit * 1024 * 1024),
        cost_estimate=pl.CostEstimate(flops=flops, bytes_accessed=moved, transcendentals=0),
    )(*args)


def dot(left, right, dims):
    return lax.dot_general(left, right, (dims, ((), ())), preferred_element_type=jnp.float32)


def halves(rows):
    high = rows.astype(jnp.bfloat16)
    low = (rows - high.astype(jnp.float32)).astype(jnp.bfloat16)
    return high, low


def pick(index, size):
    spots = lax.broadcasted_iota(jnp.int32, (size, index.shape[1]), 0)
    return (spots == index).astype(jnp.float32)


def take(chosen, table):
    high, low = halves(table)
    chosen = chosen.astype(jnp.bfloat16)
    return dot(
        jnp.concatenate([chosen, chosen], axis=0), jnp.concatenate([high, low], axis=0), LEFT
    )


def put(chosen, rows):
    high, low = halves(rows)
    chosen = chosen.astype(jnp.bfloat16)
    return dot(chosen, high, ROWS) + dot(chosen, low, ROWS)


def quarters(rows):
    size = rows.shape[-1] // 4
    return [rows[:, i * size : (i + 1) * size] for i in range(4)]


def hamilton(left, right):
    la, lb, lc, ld = left
    ra, rb, rc, rd = right
    return [
        la * ra - lb * rb - lc * rc - ld * rd,
        la * rb + lb * ra + lc * rd - ld * rc,
        la * rc - lb * rd + lc * ra + ld * rb,
        la * rd + lb * rc - lc * rb + ld * ra,
    ]


def conjugate(parts):
    return [parts[0], -parts[1], -parts[2], -parts[3]]


def join(parts):
    return jnp.concatenate(parts, axis=-1)


def gather_kernel(order, send_ref, neg_ref, entity_ref, negs_out, *refs):
    count = len(order)
    outs, (negs, *parcels) = refs[:count], refs[count : 2 * count + 1]
    rows, sends, picks, sems = refs[2 * count + 1 :]
    copies = [
        pltpu.make_async_copy(source, target, sems.at[i])
        for i, (source, target) in enumerate(
            ((entity_ref, rows), (send_ref, sends), (neg_ref, picks))
        )
    ]
    for copy in copies:
        copy.start()
    for copy in copies:
        copy.wait()
    rel_here = lax.axis_index("rel")
    slots = send_ref.shape[2]
    for i in range(neg_ref.shape[1]):
        negs[pl.ds(i, 1), :] = rows[pl.ds(picks[rel_here, i], 1), :]
    copies = [pltpu.make_async_copy(negs, negs_out, sems.at[3])]
    copies[0].start()
    for s in order:
        for core in range(2):
            peer = (2 * s + core) ^ rel_here
            for t in range(slots):
                parcels[s][pl.ds(core * slots + t, 1), :] = rows[pl.ds(sends[0, peer, t], 1), :]
        copies.append(pltpu.make_async_copy(parcels[s], outs[s], sems.at[4 + s]))
        copies[-1].start()
    for copy in copies:
        copy.wait()


def unit_parts(rows):
    parts = quarters(rows)
    inverse = lax.rsqrt(sum(part * part for part in parts))
    return [part * inverse for part in parts], inverse


def rotation_kernel(rel_index_ref, relation_ref, rot_ref):
    unit, _ = unit_parts(relation_ref[...])
    chosen = pick(rel_index_ref[...].reshape(1, -1), relation_ref.shape[0])
    rot_ref[...] = take(chosen, join(unit))


def relative(index_ref, rel_here, slots):
    index = index_ref[...].reshape(1, -1)
    return ((index // slots) ^ rel_here) * slots + index % slots


def both_picks(head_ref, tail_ref, slots, size):
    rel_here = lax.axis_index("rel")
    heads = pick(relative(head_ref, rel_here, slots), size)
    tails = pick(relative(tail_ref, rel_here, slots), size)
    return jnp.concatenate([heads, tails], axis=1)


def scores_kernel(
    slots, n_chip, head_ref, tail_ref, rot_ref, *refs
):
    arrived, (stacked, swapped) = refs[:n_chip], refs[n_chip : n_chip + 2]
    mine_ref, theirs_ref, query_ref, head_out, tail_out, pull_ref, push_ref = refs[n_chip + 2 :]
    half = mine_ref.shape[0]
    parts = []
    for s in range(n_chip):
        parts += [arrived[s][:slots], swapped[half + s * slots : half + (s + 1) * slots]]
    touched = jnp.concatenate(parts, axis=0)
    negs = jnp.concatenate([stacked[:half], swapped[:half]], axis=0)
    trips = head_ref.shape[0]
    rows = take(both_picks(head_ref, tail_ref, slots, touched.shape[0]), touched)
    head, tail = rows[:trips], rows[trips:]
    query = join(hamilton(quarters(head), quarters(rot_ref[...])))
    positive = jnp.sum(query * tail, axis=-1, keepdims=True)
    pull_ref[...] = jnp.broadcast_to(-jax.nn.sigmoid(-positive), pull_ref.shape)
    query_ref[...], head_out[...], tail_out[...] = query, head, tail
    q_high, q_low = halves(query)
    n_high, n_low = halves(negs)
    scores = dot(q_high, n_high, COLS) + dot(q_high, n_low, COLS) + dot(q_low, n_high, COLS)
    push = jax.nn.sigmoid(scores) * (1.0 / negs.shape[0])
    push_ref[...] = push
    p_high, p_low = halves(push)
    grad = dot(p_high, q_high, LEFT) + dot(p_low, q_high, LEFT) + dot(p_high, q_low, LEFT)
    middle = mine_ref.shape[0]
    mine_ref[...] = grad[:middle]
    theirs_ref[...] = grad[middle:]


def grad_kernel(slots, half, head_ref, rel_index_ref, tail_ref, relation_ref, rot_ref, *refs):
    stacked, swapped, query_ref, head_rows, tail_rows, pull_ref, push_ref = refs[:7]
    low_ref, high_ref, touched_ref = refs[7:]
    negs = jnp.concatenate([stacked[:half], swapped[:half]], axis=0)
    p_high, p_low = halves(push_ref[...])
    n_high, n_low = halves(negs)
    pulled = dot(p_high, n_high, ROWS) + dot(p_low, n_high, ROWS) + dot(p_high, n_low, ROWS)
    pull = pull_ref[:, :1]
    grad_query = quarters(pulled + pull * tail_rows[...])
    grad_head = join(hamilton(grad_query, conjugate(quarters(rot_ref[...]))))
    grad_rot = join(hamilton(conjugate(quarters(head_rows[...])), grad_query))
    grad_tail = pull * query_ref[...]
    chosen = both_picks(head_ref, tail_ref, slots, touched_ref.shape[0])
    touched_ref[...] = put(chosen, jnp.concatenate([grad_head, grad_tail], axis=0))
    unit, inverse = unit_parts(relation_ref[...])
    chosen = pick(rel_index_ref[...].reshape(1, -1), relation_ref.shape[0])
    grad_unit = quarters(put(chosen, grad_rot))
    along = sum(u * g for u, g in zip(unit, grad_unit))
    rel_grad = join([inverse * (g - u * along) for u, g in zip(unit, grad_unit)])
    middle = low_ref.shape[0]
    low_ref[...] = rel_grad[:middle]
    high_ref[...] = rel_grad[middle:]


def select_kernel(part_ref, after_ref, *refs):
    *blocks, out_ref = refs
    source = lax.axis_index("dom") ^ part_ref[0]
    picked = blocks[0][...]
    for s, ref in enumerate(blocks):
        picked = jnp.where(source == s, ref[...], picked)
    out_ref[...] = picked


def pack_kernel(slots, n_neg, mine, theirs, touched, low, high, low_ref, high_ref, *back):
    low_ref[...] = low[...]
    high_ref[...] = high[...]
    for s, ref in enumerate(back):
        block = pl.ds(s * n_neg, n_neg)
        ref[: 2 * slots] = touched[2 * s * slots : 2 * (s + 1) * slots]
        ref[2 * slots :] = mine[block] + theirs[block]


def stack_kernel(order, *refs):
    count = len(order)
    arrived, negs, out_ref = refs[:count], refs[count : 2 * count], refs[-1]
    n_neg, slots = negs[0].shape[0], arrived[0].shape[0] // 2
    for s, block, rows in zip(order, negs, arrived):
        out_ref[s * n_neg : (s + 1) * n_neg] = block[...]
        start = count * n_neg + s * slots
        out_ref[start : start + slots] = rows[slots:]


def unpack_kernel(slots, order, *refs):
    back, (neg_ref, stay_ref, cross_ref) = refs[: len(order)], refs[-3:]
    neg_ref[...] = sum(ref[2 * slots :] for ref in back)
    for s, ref in zip(order, back):
        rows = pl.ds(s * slots, slots)
        stay_ref[rows] = ref[:slots]
        cross_ref[rows] = ref[slots : 2 * slots]


def adagrad(values, history, gradient):
    history_new = history + gradient * gradient
    return values - step_size * gradient * lax.rsqrt(history_new), history_new


def entity_kernel(part_ref, send_ref, neg_ref, entity_ref, acc_ref, stay_ref, cross_ref, *refs):
    negs, (out_ref, acc_out) = refs[:-2], refs[-2:]
    rel_here = lax.axis_index("rel")
    owner = (lax.axis_index("dom") == part_ref[0]).astype(jnp.float32)
    size = entity_ref.shape[0]
    slots = send_ref.shape[2]
    neg = sum(ref[...] for ref in negs) * owner
    chosen = [pick(neg_ref[pl.ds(rel_here, 1), :], size)]
    rows = [neg]
    for k, ref in ((0, stay_ref), (1, cross_ref)):
        for s in range(send_ref.shape[1] // 2):
            peer = (2 * s + k) ^ rel_here
            chosen.append(pick(send_ref[0, pl.ds(peer, 1), :], size))
            rows.append(ref[s * slots : (s + 1) * slots])
    grad = put(jnp.concatenate(chosen, axis=1), jnp.concatenate(rows, axis=0))
    out_ref[...], acc_out[...] = adagrad(entity_ref[...], acc_ref[...], grad)


def relation_kernel(low_a, low_b, high_a, high_b, relation_ref, acc_ref, out_ref, acc_out):
    grad = jnp.concatenate([low_a[...] + low_b[...], high_a[...] + high_b[...]], axis=0)
    out_ref[...], acc_out[...] = adagrad(relation_ref[...], acc_ref[...], grad)


def shards(
    entity,
    entity_acc,
    relation,
    relation_acc,
    send_rows,
    trip_head,
    trip_rel,
    trip_tail,
    neg_part,
    neg_rows,
    *,
    n_dom,
    n_rel,
):
    ents, width = entity.shape
    rels = relation.shape[0]
    trips = trip_head.shape[0]
    slots = send_rows.shape[2]
    n_neg = neg_rows.shape[1]
    n_chip = n_rel // 2

    order = [*range(2, n_chip), *range(min(n_chip, 2))]
    own_negs, *parcels = call(
        functools.partial(gather_kernel, order),
        [(n_neg, width)] + [(2 * slots, width)] * n_chip,
        [HBM, HBM, HBM],
        (send_rows, neg_rows, entity),
        limit=60,
        out_space=HBM,
        scratch=[pltpu.VMEM((n_neg, width), jnp.float32)]
        + [pltpu.VMEM((2 * slots, width), jnp.float32)] * n_chip
        + [
            pltpu.VMEM(entity.shape, jnp.float32),
            pltpu.SMEM(send_rows.shape, jnp.int32),
            pltpu.SMEM(neg_rows.shape, jnp.int32),
            pltpu.SemaphoreType.DMA((4 + n_chip,)),
        ],
    )
    spread = [own_negs] + [exchange(own_negs, "dom", n_dom, s) for s in range(1, n_dom)]
    arrived = [parcels[0]] + [exchange(parcels[s], "rel", n_rel, 2 * s) for s in range(1, n_chip)]
    (rot,) = call(rotation_kernel, [(trips, width)], [VMEM] * 2, (trip_rel, relation))
    (picked,) = call(
        select_kernel,
        [own_negs.shape],
        [SMEM, VMEM] + [VMEM] * n_dom,
        (neg_part, rot, *spread),
    )
    negs = [picked] + [exchange(picked, "rel", n_rel, 2 * s) for s in range(1, n_chip)]
    (stacked,) = call(
        functools.partial(stack_kernel, order),
        [(n_chip * (n_neg + slots), width)],
        [VMEM] * (2 * n_chip),
        (*[arrived[s] for s in order], *[negs[s] for s in order]),
    )
    swapped = exchange(stacked, "rel", n_rel, 1)

    mine, theirs, *saved = call(
        functools.partial(scores_kernel, slots, n_chip),
        [(n_chip * n_neg, width)] * 2 + [(trips, width)] * 3 + [(trips, 128), (trips, n_rel * n_neg)],
        [VMEM] * (5 + n_chip),
        (trip_head, trip_tail, rot, *arrived, stacked, swapped),
    )
    theirs = exchange(theirs, "rel", n_rel, 1)
    low, high, touched = call(
        functools.partial(grad_kernel, slots, n_chip * n_neg),
        [(rels // 2, width)] * 2 + [(n_rel * slots, width)],
        [VMEM] * 12,
        (trip_head, trip_rel, trip_tail, relation, rot, stacked, swapped, *saved),
    )

    low, high, *back = call(
        functools.partial(pack_kernel, slots, n_neg),
        [low.shape, high.shape] + [(2 * slots + n_neg, width)] * n_chip,
        [VMEM] * 5,
        (mine, theirs, touched, low, high),
    )
    back = [back[0]] + [exchange(back[s], "rel", n_rel, 2 * s) for s in range(1, n_chip)]
    bits = [1 << b for b in range((n_dom - 1).bit_length())]
    sums = [[low], [high]]
    first = []
    for up, down in zip(bits, bits[::-1]):
        sums = [[sum(pair)] for pair in sums]
        first = first or ([sums[0][0], sums[1][0]] if len(bits) > 1 and up != bits[0] else [])
        sums[0].append(exchange(sums[0][0], "dom", n_dom, up))
        sums[1].append(exchange(sums[1][0], "dom", n_dom, down))
    neg_share, stay, cross = call(
        functools.partial(unpack_kernel, slots, order),
        [(n_neg, width)] + [(n_chip * slots, width)] * 2,
        [VMEM] * n_chip,
        [back[s] for s in order],
    )
    neg_shares = [neg_share] + [exchange(neg_share, "dom", n_dom, s) for s in range(1, n_dom)]
    cross = exchange(cross, "rel", n_rel, 1)

    new_relation, new_relation_acc = call(
        relation_kernel,
        [relation.shape] * 2,
        [VMEM] * 6,
        (*sums[0], *sums[1], relation, relation_acc),
    )

    new_entity, new_entity_acc = call(
        entity_kernel,
        [entity.shape] * 2,
        [SMEM] + [VMEM] * (6 + n_dom),
        (neg_part, send_rows, neg_rows, entity, entity_acc, stay, cross, *neg_shares),
    )
    return (new_entity, new_entity_acc, new_relation, new_relation_acc)


def solution(mesh):
    def step(*arrays):
        return shards(*arrays, n_dom=mesh.shape["dom"], n_rel=mesh.shape["rel"])

    both = ("dom", "rel")
    in_specs = (
        P(both, None),
        P(both, None),
        P("rel", None),
        P("rel", None),
        P(both, None, None),
        P(both),
        P(both),
        P(both),
        P(),
        P(),
    )
    out_specs = (P(both, None), P(both, None), P("rel", None), P("rel", None))
    return jax.shard_map(step, mesh=mesh, in_specs=in_specs, out_specs=out_specs, check_vma=False)
```

```python
import functools

import jax
import jax.numpy as jnp
from jax import lax
from jax.experimental import pallas as pl
from jax.experimental.pallas import tpu as pltpu
from jax.sharding import PartitionSpec as P

step_size = 0.05
SMEM = pl.BlockSpec(memory_space=pltpu.SMEM)
VMEM = pl.BlockSpec(memory_space=pltpu.VMEM)
HBM = pl.BlockSpec(memory_space=pltpu.HBM)
ROWS = ((1,), (0,))
COLS = ((1,), (1,))
LEFT = ((0,), (0,))


def exchange(block, axis, size, step):
    return lax.ppermute(block, axis, [(i, i ^ step) for i in range(size)])


def call(body, outs, specs, args, flops=0, scratch=(), limit=40 * 1024):
    shapes = [jax.ShapeDtypeStruct(shape, jnp.float32) for shape in outs]
    moved = 4 * sum(int(a.size) for a in args) + 4 * sum(int(s.size) for s in shapes)
    return pl.pallas_call(
        body,
        out_shape=shapes,
        in_specs=specs,
        out_specs=[VMEM] * len(shapes),
        scratch_shapes=scratch,
        compiler_params=pltpu.CompilerParams(vmem_limit_bytes=limit * 1024),
        cost_estimate=pl.CostEstimate(flops=flops, bytes_accessed=moved, transcendentals=0),
    )(*args)


def dot(left, right, dims):
    return lax.dot_general(left, right, (dims, ((), ())), preferred_element_type=jnp.float32)


def halves(rows):
    high = rows.astype(jnp.bfloat16)
    low = (rows - high.astype(jnp.float32)).astype(jnp.bfloat16)
    return high, low


def pick(index, size):
    spots = lax.broadcasted_iota(jnp.int32, (size, index.shape[1]), 0)
    return (spots == index).astype(jnp.float32)


def take(chosen, table):
    high, low = halves(table)
    chosen = chosen.astype(jnp.bfloat16)
    return dot(
        jnp.concatenate([chosen, chosen], axis=0), jnp.concatenate([high, low], axis=0), LEFT
    )


def put(chosen, rows):
    high, low = halves(rows)
    chosen = chosen.astype(jnp.bfloat16)
    return dot(chosen, high, ROWS) + dot(chosen, low, ROWS)


def quarters(rows):
    size = rows.shape[-1] // 4
    return [rows[:, i * size : (i + 1) * size] for i in range(4)]


def hamilton(left, right):
    la, lb, lc, ld = left
    ra, rb, rc, rd = right
    return [
        la * ra - lb * rb - lc * rc - ld * rd,
        la * rb + lb * ra + lc * rd - ld * rc,
        la * rc - lb * rd + lc * ra + ld * rb,
        la * rd + lb * rc - lc * rb + ld * ra,
    ]


def conjugate(parts):
    return [parts[0], -parts[1], -parts[2], -parts[3]]


def join(parts):
    return jnp.concatenate(parts, axis=-1)


def gather_kernel(send_ref, neg_ref, entity_ref, negs, *refs):
    *parcels, rows, sends, picks, sems = refs
    copies = [
        pltpu.make_async_copy(source, target, sems.at[i])
        for i, (source, target) in enumerate(
            ((entity_ref, rows), (send_ref, sends), (neg_ref, picks))
        )
    ]
    for copy in copies:
        copy.start()
    for copy in copies:
        copy.wait()
    rel_here = lax.axis_index("rel")
    slots = send_ref.shape[2]
    for i in range(neg_ref.shape[1]):
        negs[pl.ds(i, 1), :] = rows[pl.ds(picks[rel_here, i], 1), :]
    for s, ref in enumerate(parcels):
        for core in range(2):
            peer = (2 * s + core) ^ rel_here
            for t in range(slots):
                ref[pl.ds(core * slots + t, 1), :] = rows[pl.ds(sends[0, peer, t], 1), :]


def unit_parts(rows):
    parts = quarters(rows)
    inverse = lax.rsqrt(sum(part * part for part in parts))
    return [part * inverse for part in parts], inverse


def rotation_kernel(rel_index_ref, relation_ref, rot_ref):
    unit, _ = unit_parts(relation_ref[...])
    chosen = pick(rel_index_ref[...].reshape(1, -1), relation_ref.shape[0])
    rot_ref[...] = take(chosen, join(unit))


def relative(index_ref, rel_here, slots):
    index = index_ref[...].reshape(1, -1)
    return ((index // slots) ^ rel_here) * slots + index % slots


def both_picks(head_ref, tail_ref, slots, size):
    rel_here = lax.axis_index("rel")
    heads = pick(relative(head_ref, rel_here, slots), size)
    tails = pick(relative(tail_ref, rel_here, slots), size)
    return jnp.concatenate([heads, tails], axis=1)


def scores_kernel(
    slots, n_chip, head_ref, tail_ref, rot_ref, *refs
):
    arrived, (stacked, swapped) = refs[:n_chip], refs[n_chip : n_chip + 2]
    mine_ref, theirs_ref, query_ref, head_out, tail_out, pull_ref, push_ref = refs[n_chip + 2 :]
    half = mine_ref.shape[0]
    parts = []
    for s in range(n_chip):
        parts += [arrived[s][:slots], swapped[half + s * slots : half + (s + 1) * slots]]
    touched = jnp.concatenate(parts, axis=0)
    negs = jnp.concatenate([stacked[:half], swapped[:half]], axis=0)
    trips = head_ref.shape[0]
    rows = take(both_picks(head_ref, tail_ref, slots, touched.shape[0]), touched)
    head, tail = rows[:trips], rows[trips:]
    query = join(hamilton(quarters(head), quarters(rot_ref[...])))
    positive = jnp.sum(query * tail, axis=-1, keepdims=True)
    pull_ref[...] = jnp.broadcast_to(-jax.nn.sigmoid(-positive), pull_ref.shape)
    query_ref[...], head_out[...], tail_out[...] = query, head, tail
    q_high, q_low = halves(query)
    n_high, n_low = halves(negs)
    scores = dot(
        jnp.concatenate([n_high, n_low, n_high], axis=1),
        jnp.concatenate([q_high, q_high, q_low], axis=1),
        COLS,
    )
    push = jax.nn.sigmoid(scores) * (1.0 / negs.shape[0])
    push_ref[...] = push
    p_high, p_low = halves(push)
    grad = dot(
        jnp.concatenate([p_high, p_low, p_high], axis=1),
        jnp.concatenate([q_high, q_high, q_low], axis=0),
        ROWS,
    )
    middle = mine_ref.shape[0]
    mine_ref[...] = grad[:middle]
    theirs_ref[...] = grad[middle:]


def grad_kernel(slots, half, head_ref, rel_index_ref, tail_ref, relation_ref, rot_ref, *refs):
    stacked, swapped, query_ref, head_rows, tail_rows, pull_ref, push_ref = refs[:7]
    low_ref, high_ref, touched_ref = refs[7:]
    negs = jnp.concatenate([stacked[:half], swapped[:half]], axis=0)
    p_high, p_low = halves(push_ref[...])
    n_high, n_low = halves(negs)
    pulled = dot(p_high, n_high, LEFT) + dot(p_low, n_high, LEFT) + dot(p_high, n_low, LEFT)
    pull = pull_ref[:, :1]
    grad_query = quarters(pulled + pull * tail_rows[...])
    grad_head = join(hamilton(grad_query, conjugate(quarters(rot_ref[...]))))
    grad_rot = join(hamilton(conjugate(quarters(head_rows[...])), grad_query))
    grad_tail = pull * query_ref[...]
    chosen = both_picks(head_ref, tail_ref, slots, touched_ref.shape[0])
    touched_ref[...] = put(chosen, jnp.concatenate([grad_head, grad_tail], axis=0))
    unit, inverse = unit_parts(relation_ref[...])
    chosen = pick(rel_index_ref[...].reshape(1, -1), relation_ref.shape[0])
    grad_unit = quarters(put(chosen, grad_rot))
    along = sum(u * g for u, g in zip(unit, grad_unit))
    rel_grad = join([inverse * (g - u * along) for u, g in zip(unit, grad_unit)])
    middle = low_ref.shape[0]
    low_ref[...] = rel_grad[:middle]
    high_ref[...] = rel_grad[middle:]


def select_kernel(part_ref, after_ref, *refs):
    *blocks, out_ref = refs
    source = lax.axis_index("dom") ^ part_ref[0]
    picked = blocks[0][...]
    for s, ref in enumerate(blocks):
        picked = jnp.where(source == s, ref[...], picked)
    out_ref[...] = picked


def pack_kernel(slots, n_neg, mine, theirs, touched, low, high, low_ref, high_ref, *back):
    low_ref[...] = low[...]
    high_ref[...] = high[...]
    for s, ref in enumerate(back):
        block = pl.ds(s * n_neg, n_neg)
        ref[: 2 * slots] = touched[2 * s * slots : 2 * (s + 1) * slots]
        ref[2 * slots :] = mine[block] + theirs[block]


def stack_kernel(order, *refs):
    count = len(order)
    arrived, negs, out_ref = refs[:count], refs[count : 2 * count], refs[-1]
    n_neg, slots = negs[0].shape[0], arrived[0].shape[0] // 2
    for s, block, rows in zip(order, negs, arrived):
        out_ref[s * n_neg : (s + 1) * n_neg] = block[...]
        start = count * n_neg + s * slots
        out_ref[start : start + slots] = rows[slots:]


def unpack_kernel(slots, order, *refs):
    back, (neg_ref, stay_ref, cross_ref) = refs[: len(order)], refs[-3:]
    neg_ref[...] = sum(ref[2 * slots :] for ref in back)
    for s, ref in zip(order, back):
        rows = pl.ds(s * slots, slots)
        stay_ref[rows] = ref[:slots]
        cross_ref[rows] = ref[slots : 2 * slots]


def adagrad(values, history, gradient):
    history_new = history + gradient * gradient
    return values - step_size * gradient * lax.rsqrt(history_new), history_new


def entity_kernel(part_ref, send_ref, neg_ref, entity_ref, acc_ref, stay_ref, cross_ref, *refs):
    negs, (out_ref, acc_out) = refs[:-2], refs[-2:]
    rel_here = lax.axis_index("rel")
    owner = (lax.axis_index("dom") == part_ref[0]).astype(jnp.float32)
    size = entity_ref.shape[0]
    slots = send_ref.shape[2]
    neg = sum(ref[...] for ref in negs) * owner
    chosen = [pick(neg_ref[pl.ds(rel_here, 1), :], size)]
    rows = [neg]
    for k, ref in ((0, stay_ref), (1, cross_ref)):
        for s in range(send_ref.shape[1] // 2):
            peer = (2 * s + k) ^ rel_here
            chosen.append(pick(send_ref[0, pl.ds(peer, 1), :], size))
            rows.append(ref[s * slots : (s + 1) * slots])
    grad = put(jnp.concatenate(chosen, axis=1), jnp.concatenate(rows, axis=0))
    out_ref[...], acc_out[...] = adagrad(entity_ref[...], acc_ref[...], grad)


def relation_kernel(low_a, low_b, high_a, high_b, relation_ref, acc_ref, out_ref, acc_out):
    grad = jnp.concatenate([low_a[...] + low_b[...], high_a[...] + high_b[...]], axis=0)
    out_ref[...], acc_out[...] = adagrad(relation_ref[...], acc_ref[...], grad)


def shards(
    entity,
    entity_acc,
    relation,
    relation_acc,
    send_rows,
    trip_head,
    trip_rel,
    trip_tail,
    neg_part,
    neg_rows,
    *,
    n_dom,
    n_rel,
):
    ents, width = entity.shape
    rels = relation.shape[0]
    trips = trip_head.shape[0]
    slots = send_rows.shape[2]
    n_neg = neg_rows.shape[1]
    n_chip = n_rel // 2

    order = [*range(2, n_chip), *range(min(n_chip, 2))]
    own_negs, *parcels = call(
        gather_kernel,
        [(n_neg, width)] + [(2 * slots, width)] * n_chip,
        [HBM, HBM, HBM],
        (send_rows, neg_rows, entity),
        limit=60 * 1024,
        scratch=[
            pltpu.VMEM(entity.shape, jnp.float32),
            pltpu.SMEM(send_rows.shape, jnp.int32),
            pltpu.SMEM(neg_rows.shape, jnp.int32),
            pltpu.SemaphoreType.DMA((3,)),
        ],
    )
    spread = [own_negs] + [exchange(own_negs, "dom", n_dom, s) for s in range(1, n_dom)]
    arrived = [parcels[0]] + [exchange(parcels[s], "rel", n_rel, 2 * s) for s in range(1, n_chip)]
    (rot,) = call(rotation_kernel, [(trips, width)], [VMEM] * 2, (trip_rel, relation))
    (picked,) = call(
        select_kernel,
        [own_negs.shape],
        [SMEM, VMEM] + [VMEM] * n_dom,
        (neg_part, rot, *spread),
    )
    negs = [picked] + [exchange(picked, "rel", n_rel, 2 * s) for s in range(1, n_chip)]
    (stacked,) = call(
        functools.partial(stack_kernel, order),
        [(n_chip * (n_neg + slots), width)],
        [VMEM] * (2 * n_chip),
        (*[arrived[s] for s in order], *[negs[s] for s in order]),
    )
    swapped = exchange(stacked, "rel", n_rel, 1)

    mine, theirs, *saved = call(
        functools.partial(scores_kernel, slots, n_chip),
        [(n_chip * n_neg, width)] * 2 + [(trips, width)] * 3 + [(trips, 128), (n_rel * n_neg, trips)],
        [VMEM] * (5 + n_chip),
        (trip_head, trip_tail, rot, *arrived, stacked, swapped),
    )
    theirs = exchange(theirs, "rel", n_rel, 1)
    low, high, touched = call(
        functools.partial(grad_kernel, slots, n_chip * n_neg),
        [(rels // 2, width)] * 2 + [(n_rel * slots, width)],
        [VMEM] * 12,
        (trip_head, trip_rel, trip_tail, relation, rot, stacked, swapped, *saved),
    )

    low, high, *back = call(
        functools.partial(pack_kernel, slots, n_neg),
        [low.shape, high.shape] + [(2 * slots + n_neg, width)] * n_chip,
        [VMEM] * 5,
        (mine, theirs, touched, low, high),
    )
    back = [back[0]] + [exchange(back[s], "rel", n_rel, 2 * s) for s in range(1, n_chip)]
    bits = [1 << b for b in range((n_dom - 1).bit_length())]
    sums = [[low], [high]]
    first = []
    for up, down in zip(bits, bits[::-1]):
        sums = [[sum(pair)] for pair in sums]
        first = first or ([sums[0][0], sums[1][0]] if len(bits) > 1 and up != bits[0] else [])
        sums[0].append(exchange(sums[0][0], "dom", n_dom, up))
        sums[1].append(exchange(sums[1][0], "dom", n_dom, down))
    back_order = [*range(2, n_chip, 2), *range(min(n_chip, 2))[::-1], *range(3, n_chip, 2)]
    neg_share, stay, cross = call(
        functools.partial(unpack_kernel, slots, back_order),
        [(n_neg, width)] + [(n_chip * slots, width)] * 2,
        [VMEM] * n_chip,
        [back[s] for s in back_order],
    )
    neg_shares = [neg_share] + [exchange(neg_share, "dom", n_dom, s) for s in range(1, n_dom)]
    cross = exchange(cross, "rel", n_rel, 1)

    new_relation, new_relation_acc = call(
        relation_kernel,
        [relation.shape] * 2,
        [VMEM] * 6,
        (*sums[0], *sums[1], relation, relation_acc),
    )

    new_entity, new_entity_acc = call(
        entity_kernel,
        [entity.shape] * 2,
        [SMEM] + [VMEM] * (6 + n_dom),
        (neg_part, send_rows, neg_rows, entity, entity_acc, stay, cross, *neg_shares),
    )
    return (new_entity, new_entity_acc, new_relation, new_relation_acc)


def solution(mesh):
    def step(*arrays):
        return shards(*arrays, n_dom=mesh.shape["dom"], n_rel=mesh.shape["rel"])

    both = ("dom", "rel")
    in_specs = (
        P(both, None),
        P(both, None),
        P("rel", None),
        P("rel", None),
        P(both, None, None),
        P(both),
        P(both),
        P(both),
        P(),
        P(),
    )
    out_specs = (P(both, None), P(both, None), P("rel", None), P("rel", None))
    return jax.shard_map(step, mesh=mesh, in_specs=in_specs, out_specs=out_specs, check_vma=False)
```

```python
import functools

import jax
import jax.numpy as jnp
from jax import lax
from jax.experimental import pallas as pl
from jax.experimental.pallas import tpu as pltpu
from jax.sharding import PartitionSpec as P

step_size = 0.05
SMEM = pl.BlockSpec(memory_space=pltpu.SMEM)
VMEM = pl.BlockSpec(memory_space=pltpu.VMEM)
HBM = pl.BlockSpec(memory_space=pltpu.HBM)
ROWS = ((1,), (0,))
COLS = ((1,), (1,))
LEFT = ((0,), (0,))


def exchange(block, axis, size, step):
    return lax.ppermute(block, axis, [(i, i ^ step) for i in range(size)])


def call(body, outs, specs, args, flops=0, scratch=(), limit=40 * 1024):
    shapes = [jax.ShapeDtypeStruct(shape, jnp.float32) for shape in outs]
    moved = 4 * sum(int(a.size) for a in args) + 4 * sum(int(s.size) for s in shapes)
    return pl.pallas_call(
        body,
        out_shape=shapes,
        in_specs=specs,
        out_specs=[VMEM] * len(shapes),
        scratch_shapes=scratch,
        compiler_params=pltpu.CompilerParams(vmem_limit_bytes=limit * 1024),
        cost_estimate=pl.CostEstimate(flops=flops, bytes_accessed=moved, transcendentals=0),
    )(*args)


def dot(left, right, dims):
    return lax.dot_general(left, right, (dims, ((), ())), preferred_element_type=jnp.float32)


def halves(rows):
    high = rows.astype(jnp.bfloat16)
    low = (rows - high.astype(jnp.float32)).astype(jnp.bfloat16)
    return high, low


def pick(index, size):
    spots = lax.broadcasted_iota(jnp.int32, (size, index.shape[1]), 0)
    return (spots == index).astype(jnp.float32)


def take(chosen, table):
    high, low = halves(table)
    chosen = chosen.astype(jnp.bfloat16)
    return dot(
        jnp.concatenate([chosen, chosen], axis=0), jnp.concatenate([high, low], axis=0), LEFT
    )


def put(chosen, rows):
    high, low = halves(rows)
    chosen = chosen.astype(jnp.bfloat16)
    return dot(chosen, high, ROWS) + dot(chosen, low, ROWS)


def quarters(rows):
    size = rows.shape[-1] // 4
    return [rows[:, i * size : (i + 1) * size] for i in range(4)]


def hamilton(left, right):
    la, lb, lc, ld = left
    ra, rb, rc, rd = right
    return [
        la * ra - lb * rb - lc * rc - ld * rd,
        la * rb + lb * ra + lc * rd - ld * rc,
        la * rc - lb * rd + lc * ra + ld * rb,
        la * rd + lb * rc - lc * rb + ld * ra,
    ]


def conjugate(parts):
    return [parts[0], -parts[1], -parts[2], -parts[3]]


def join(parts):
    return jnp.concatenate(parts, axis=-1)


def gather_kernel(send_ref, neg_ref, entity_ref, negs, *refs):
    *parcels, rows, sends, picks, sems = refs
    copies = [
        pltpu.make_async_copy(source, target, sems.at[i])
        for i, (source, target) in enumerate(
            ((entity_ref, rows), (send_ref, sends), (neg_ref, picks))
        )
    ]
    for copy in copies:
        copy.start()
    for copy in copies:
        copy.wait()
    rel_here = lax.axis_index("rel")
    slots = send_ref.shape[2]
    for i in range(neg_ref.shape[1]):
        negs[pl.ds(i, 1), :] = rows[pl.ds(picks[rel_here, i], 1), :]
    for s, ref in enumerate(parcels):
        for core in range(2):
            peer = (2 * s + core) ^ rel_here
            for t in range(slots):
                ref[pl.ds(core * slots + t, 1), :] = rows[pl.ds(sends[0, peer, t], 1), :]


def unit_parts(rows):
    parts = quarters(rows)
    inverse = lax.rsqrt(sum(part * part for part in parts))
    return [part * inverse for part in parts], inverse


def rotation_kernel(rel_index_ref, relation_ref, rot_ref):
    unit, _ = unit_parts(relation_ref[...])
    chosen = pick(rel_index_ref[...].reshape(1, -1), relation_ref.shape[0])
    rot_ref[...] = take(chosen, join(unit))


def relative(index_ref, rel_here, slots):
    index = index_ref[...].reshape(1, -1)
    return ((index // slots) ^ rel_here) * slots + index % slots


def both_picks(head_ref, tail_ref, slots, size):
    rel_here = lax.axis_index("rel")
    heads = pick(relative(head_ref, rel_here, slots), size)
    tails = pick(relative(tail_ref, rel_here, slots), size)
    return jnp.concatenate([heads, tails], axis=1)


def scores_kernel(
    slots, n_chip, head_ref, tail_ref, rot_ref, *refs
):
    arrived, (stacked, swapped) = refs[:n_chip], refs[n_chip : n_chip + 2]
    mine_ref, theirs_ref, query_ref, head_out, tail_out, pull_ref, push_ref = refs[n_chip + 2 :]
    half = mine_ref.shape[0]
    parts = []
    for s in range(n_chip):
        parts += [arrived[s][:slots], swapped[half + s * slots : half + (s + 1) * slots]]
    touched = jnp.concatenate(parts, axis=0)
    negs = jnp.concatenate([stacked[:half], swapped[:half]], axis=0)
    trips = head_ref.shape[0]
    rows = take(both_picks(head_ref, tail_ref, slots, touched.shape[0]), touched)
    head, tail = rows[:trips], rows[trips:]
    query = join(hamilton(quarters(head), quarters(rot_ref[...])))
    positive = jnp.sum(query * tail, axis=-1, keepdims=True)
    pull_ref[...] = jnp.broadcast_to(-jax.nn.sigmoid(-positive), pull_ref.shape)
    query_ref[...], head_out[...], tail_out[...] = query, head, tail
    q_high, q_low = halves(query)
    n_high, n_low = halves(negs)
    scores = dot(
        jnp.concatenate([n_high, n_low, n_high], axis=1),
        jnp.concatenate([q_high, q_high, q_low], axis=1),
        COLS,
    )
    push = jax.nn.sigmoid(scores) * (1.0 / negs.shape[0])
    push_ref[...] = push
    p_high, p_low = halves(push)
    grad = dot(
        jnp.concatenate([p_high, p_low, p_high], axis=1),
        jnp.concatenate([q_high, q_high, q_low], axis=0),
        ROWS,
    )
    middle = mine_ref.shape[0]
    mine_ref[...] = grad[:middle]
    theirs_ref[...] = grad[middle:]


def grad_kernel(slots, half, head_ref, rel_index_ref, tail_ref, relation_ref, rot_ref, *refs):
    stacked, swapped, query_ref, head_rows, tail_rows, pull_ref, push_ref = refs[:7]
    low_ref, high_ref, touched_ref = refs[7:]
    negs = jnp.concatenate([stacked[:half], swapped[:half]], axis=0)
    p_high, p_low = halves(push_ref[...])
    n_high, n_low = halves(negs)
    pulled = dot(p_high, n_high, LEFT) + dot(p_low, n_high, LEFT) + dot(p_high, n_low, LEFT)
    pull = pull_ref[:, :1]
    grad_query = quarters(pulled + pull * tail_rows[...])
    grad_head = join(hamilton(grad_query, conjugate(quarters(rot_ref[...]))))
    grad_rot = join(hamilton(conjugate(quarters(head_rows[...])), grad_query))
    grad_tail = pull * query_ref[...]
    chosen = both_picks(head_ref, tail_ref, slots, touched_ref.shape[0])
    touched_ref[...] = put(chosen, jnp.concatenate([grad_head, grad_tail], axis=0))
    unit, inverse = unit_parts(relation_ref[...])
    chosen = pick(rel_index_ref[...].reshape(1, -1), relation_ref.shape[0])
    grad_unit = quarters(put(chosen, grad_rot))
    along = sum(u * g for u, g in zip(unit, grad_unit))
    rel_grad = join([inverse * (g - u * along) for u, g in zip(unit, grad_unit)])
    middle = low_ref.shape[0]
    low_ref[...] = rel_grad[:middle]
    high_ref[...] = rel_grad[middle:]


def select_kernel(part_ref, after_ref, *refs):
    blocks, out_ref = refs[: lax.axis_size("dom")], refs[-1]
    source = lax.axis_index("dom") ^ part_ref[0]
    picked = blocks[0][...]
    for s, ref in enumerate(blocks):
        picked = jnp.where(source == s, ref[...], picked)
    out_ref[...] = picked


def pack_kernel(slots, n_neg, mine, theirs, touched, low, high, low_ref, high_ref, *back):
    low_ref[...] = low[...]
    high_ref[...] = high[...]
    for s, ref in enumerate(back):
        block = pl.ds(s * n_neg, n_neg)
        ref[: 2 * slots] = touched[2 * s * slots : 2 * (s + 1) * slots]
        ref[2 * slots :] = mine[block] + theirs[block]


def stack_kernel(order, neg_order, *refs):
    count = len(order)
    arrived, negs, out_ref = refs[:count], refs[count : 2 * count], refs[-1]
    n_neg, slots = negs[0].shape[0], arrived[0].shape[0] // 2
    for s, block in zip(neg_order, negs):
        out_ref[s * n_neg : (s + 1) * n_neg] = block[...]
    for s, rows in zip(order, arrived):
        start = count * n_neg + s * slots
        out_ref[start : start + slots] = rows[slots:]


def unpack_kernel(slots, order, *refs):
    back, (neg_ref, stay_ref, cross_ref) = refs[: len(order)], refs[-3:]
    neg_ref[...] = sum(ref[2 * slots :] for ref in back)
    for s, ref in zip(order, back):
        rows = pl.ds(s * slots, slots)
        stay_ref[rows] = ref[:slots]
        cross_ref[rows] = ref[slots : 2 * slots]


def adagrad(values, history, gradient):
    history_new = history + gradient * gradient
    return values - step_size * gradient * lax.rsqrt(history_new), history_new


def entity_kernel(part_ref, send_ref, neg_ref, entity_ref, acc_ref, stay_ref, cross_ref, *refs):
    negs, (out_ref, acc_out) = refs[:-2], refs[-2:]
    rel_here = lax.axis_index("rel")
    owner = (lax.axis_index("dom") == part_ref[0]).astype(jnp.float32)
    size = entity_ref.shape[0]
    slots = send_ref.shape[2]
    neg = sum(ref[...] for ref in negs) * owner
    chosen = [pick(neg_ref[pl.ds(rel_here, 1), :], size)]
    rows = [neg]
    for k, ref in ((0, stay_ref), (1, cross_ref)):
        for s in range(send_ref.shape[1] // 2):
            peer = (2 * s + k) ^ rel_here
            chosen.append(pick(send_ref[0, pl.ds(peer, 1), :], size))
            rows.append(ref[s * slots : (s + 1) * slots])
    grad = put(jnp.concatenate(chosen, axis=1), jnp.concatenate(rows, axis=0))
    out_ref[...], acc_out[...] = adagrad(entity_ref[...], acc_ref[...], grad)


def relation_kernel(low_a, low_b, high_a, high_b, relation_ref, acc_ref, out_ref, acc_out):
    grad = jnp.concatenate([low_a[...] + low_b[...], high_a[...] + high_b[...]], axis=0)
    out_ref[...], acc_out[...] = adagrad(relation_ref[...], acc_ref[...], grad)


def shards(
    entity,
    entity_acc,
    relation,
    relation_acc,
    send_rows,
    trip_head,
    trip_rel,
    trip_tail,
    neg_part,
    neg_rows,
    *,
    n_dom,
    n_rel,
):
    ents, width = entity.shape
    rels = relation.shape[0]
    trips = trip_head.shape[0]
    slots = send_rows.shape[2]
    n_neg = neg_rows.shape[1]
    n_chip = n_rel // 2

    order = [*range(2, n_chip), *range(min(n_chip, 2))]
    own_negs, *parcels = call(
        gather_kernel,
        [(n_neg, width)] + [(2 * slots, width)] * n_chip,
        [HBM, HBM, HBM],
        (send_rows, neg_rows, entity),
        limit=60 * 1024,
        scratch=[
            pltpu.VMEM(entity.shape, jnp.float32),
            pltpu.SMEM(send_rows.shape, jnp.int32),
            pltpu.SMEM(neg_rows.shape, jnp.int32),
            pltpu.SemaphoreType.DMA((3,)),
        ],
    )
    spread = [own_negs] + [exchange(own_negs, "dom", n_dom, s) for s in range(1, n_dom)]
    arrived = [parcels[0]] + [exchange(parcels[s], "rel", n_rel, 2 * s) for s in range(1, n_chip)]
    (rot,) = call(rotation_kernel, [(trips, width)], [VMEM] * 2, (trip_rel, relation))
    (picked,) = call(
        select_kernel,
        [own_negs.shape],
        [SMEM, VMEM] + [VMEM] * (n_dom + len(arrived[1:2])),
        (neg_part, rot, *spread, *arrived[1:2]),
    )
    negs = [picked] + [exchange(picked, "rel", n_rel, 2 * s) for s in range(1, n_chip)]
    neg_order = [*range(2, n_chip)][::-1] + [*range(min(n_chip, 2))]
    (stacked,) = call(
        functools.partial(stack_kernel, order, neg_order),
        [(n_chip * (n_neg + slots), width)],
        [VMEM] * (2 * n_chip),
        (*[arrived[s] for s in order], *[negs[s] for s in neg_order]),
    )
    swapped = exchange(stacked, "rel", n_rel, 1)

    mine, theirs, *saved = call(
        functools.partial(scores_kernel, slots, n_chip),
        [(n_chip * n_neg, width)] * 2 + [(trips, width)] * 3 + [(trips, 128), (n_rel * n_neg, trips)],
        [VMEM] * (5 + n_chip),
        (trip_head, trip_tail, rot, *arrived, stacked, swapped),
    )
    theirs = exchange(theirs, "rel", n_rel, 1)
    low, high, touched = call(
        functools.partial(grad_kernel, slots, n_chip * n_neg),
        [(rels // 2, width)] * 2 + [(n_rel * slots, width)],
        [VMEM] * 12,
        (trip_head, trip_rel, trip_tail, relation, rot, stacked, swapped, *saved),
    )

    low, high, *back = call(
        functools.partial(pack_kernel, slots, n_neg),
        [low.shape, high.shape] + [(2 * slots + n_neg, width)] * n_chip,
        [VMEM] * 5,
        (mine, theirs, touched, low, high),
    )
    back = [back[0]] + [exchange(back[s], "rel", n_rel, 2 * s) for s in range(1, n_chip)]
    bits = [1 << b for b in range((n_dom - 1).bit_length())]
    sums = [[low], [high]]
    first = []
    for up, down in zip(bits, bits[::-1]):
        sums = [[sum(pair)] for pair in sums]
        first = first or ([sums[0][0], sums[1][0]] if len(bits) > 1 and up != bits[0] else [])
        sums[0].append(exchange(sums[0][0], "dom", n_dom, up))
        sums[1].append(exchange(sums[1][0], "dom", n_dom, down))
    back_order = [*range(2, n_chip, 2), *range(min(n_chip, 2))[::-1], *range(3, n_chip, 2)]
    neg_share, stay, cross = call(
        functools.partial(unpack_kernel, slots, back_order),
        [(n_neg, width)] + [(n_chip * slots, width)] * 2,
        [VMEM] * n_chip,
        [back[s] for s in back_order],
    )
    neg_shares = [neg_share] + [exchange(neg_share, "dom", n_dom, s) for s in range(1, n_dom)]
    cross = exchange(cross, "rel", n_rel, 1)

    new_relation, new_relation_acc = call(
        relation_kernel,
        [relation.shape] * 2,
        [VMEM] * 6,
        (*sums[0], *sums[1], relation, relation_acc),
    )

    new_entity, new_entity_acc = call(
        entity_kernel,
        [entity.shape] * 2,
        [SMEM] + [VMEM] * (6 + n_dom),
        (neg_part, send_rows, neg_rows, entity, entity_acc, stay, cross, *neg_shares),
    )
    return (new_entity, new_entity_acc, new_relation, new_relation_acc)


def solution(mesh):
    def step(*arrays):
        return shards(*arrays, n_dom=mesh.shape["dom"], n_rel=mesh.shape["rel"])

    both = ("dom", "rel")
    in_specs = (
        P(both, None),
        P(both, None),
        P("rel", None),
        P("rel", None),
        P(both, None, None),
        P(both),
        P(both),
        P(both),
        P(),
        P(),
    )
    out_specs = (P(both, None), P(both, None), P("rel", None), P("rel", None))
    return jax.shard_map(step, mesh=mesh, in_specs=in_specs, out_specs=out_specs, check_vma=False)
```

```python
import functools

import jax
import jax.numpy as jnp
from jax import lax
from jax.experimental import pallas as pl
from jax.experimental.pallas import tpu as pltpu
from jax.sharding import PartitionSpec as P

step_size = 0.05
SMEM = pl.BlockSpec(memory_space=pltpu.SMEM)
VMEM = pl.BlockSpec(memory_space=pltpu.VMEM)
HBM = pl.BlockSpec(memory_space=pltpu.HBM)
ROWS = ((1,), (0,))
COLS = ((1,), (1,))
LEFT = ((0,), (0,))


def exchange(block, axis, size, step):
    return lax.ppermute(block, axis, [(i, i ^ step) for i in range(size)])


def cross_exchange(block, n_dom, n_rel, even, odd):
    pairs = []
    for i in range(n_dom):
        for r in range(n_rel):
            pairs.append((i * n_rel + r, (i ^ (odd if r % 2 else even)) * n_rel + r))
    return lax.ppermute(block, ("dom", "rel"), pairs)


def call(body, outs, specs, args, flops=0, scratch=(), limit=40 * 1024):
    shapes = [jax.ShapeDtypeStruct(shape, jnp.float32) for shape in outs]
    moved = 4 * sum(int(a.size) for a in args) + 4 * sum(int(s.size) for s in shapes)
    return pl.pallas_call(
        body,
        out_shape=shapes,
        in_specs=specs,
        out_specs=[VMEM] * len(shapes),
        scratch_shapes=scratch,
        compiler_params=pltpu.CompilerParams(vmem_limit_bytes=limit * 1024),
        cost_estimate=pl.CostEstimate(flops=flops, bytes_accessed=moved, transcendentals=0),
    )(*args)


def dot(left, right, dims):
    return lax.dot_general(left, right, (dims, ((), ())), preferred_element_type=jnp.float32)


def halves(rows):
    high = rows.astype(jnp.bfloat16)
    low = (rows - high.astype(jnp.float32)).astype(jnp.bfloat16)
    return high, low


def pick(index, size):
    spots = lax.broadcasted_iota(jnp.int32, (size, index.shape[1]), 0)
    return (spots == index).astype(jnp.float32)


def take(chosen, table):
    high, low = halves(table)
    chosen = chosen.astype(jnp.bfloat16)
    return dot(
        jnp.concatenate([chosen, chosen], axis=0), jnp.concatenate([high, low], axis=0), LEFT
    )


def put(chosen, rows):
    high, low = halves(rows)
    chosen = chosen.astype(jnp.bfloat16)
    return dot(chosen, high, ROWS) + dot(chosen, low, ROWS)


def quarters(rows):
    size = rows.shape[-1] // 4
    return [rows[:, i * size : (i + 1) * size] for i in range(4)]


def hamilton(left, right):
    la, lb, lc, ld = left
    ra, rb, rc, rd = right
    return [
        la * ra - lb * rb - lc * rc - ld * rd,
        la * rb + lb * ra + lc * rd - ld * rc,
        la * rc - lb * rd + lc * ra + ld * rb,
        la * rd + lb * rc - lc * rb + ld * ra,
    ]


def conjugate(parts):
    return [parts[0], -parts[1], -parts[2], -parts[3]]


def join(parts):
    return jnp.concatenate(parts, axis=-1)


def gather_kernel(send_ref, neg_ref, entity_ref, negs, *refs):
    *parcels, rows, sends, picks, sems = refs
    copies = [
        pltpu.make_async_copy(source, target, sems.at[i])
        for i, (source, target) in enumerate(
            ((entity_ref, rows), (send_ref, sends), (neg_ref, picks))
        )
    ]
    for copy in copies:
        copy.start()
    for copy in copies:
        copy.wait()
    rel_here = lax.axis_index("rel")
    slots = send_ref.shape[2]
    for i in range(neg_ref.shape[1]):
        negs[pl.ds(i, 1), :] = rows[pl.ds(picks[rel_here, i], 1), :]
    for s, ref in enumerate(parcels):
        for core in range(2):
            peer = (2 * s + core) ^ rel_here
            for t in range(slots):
                ref[pl.ds(core * slots + t, 1), :] = rows[pl.ds(sends[0, peer, t], 1), :]


def unit_parts(rows):
    parts = quarters(rows)
    inverse = lax.rsqrt(sum(part * part for part in parts))
    return [part * inverse for part in parts], inverse


def rotation_kernel(rel_index_ref, relation_ref, rot_ref):
    unit, _ = unit_parts(relation_ref[...])
    chosen = pick(rel_index_ref[...].reshape(1, -1), relation_ref.shape[0])
    rot_ref[...] = take(chosen, join(unit))


def relative(index_ref, rel_here, slots):
    index = index_ref[...].reshape(1, -1)
    return ((index // slots) ^ rel_here) * slots + index % slots


def both_picks(head_ref, tail_ref, slots, size):
    rel_here = lax.axis_index("rel")
    heads = pick(relative(head_ref, rel_here, slots), size)
    tails = pick(relative(tail_ref, rel_here, slots), size)
    return jnp.concatenate([heads, tails], axis=1)


def scores_kernel(
    slots, n_chip, head_ref, tail_ref, rot_ref, *refs
):
    arrived, (stacked, swapped) = refs[:n_chip], refs[n_chip : n_chip + 2]
    mine_ref, theirs_ref, query_ref, head_out, tail_out, pull_ref, push_ref = refs[n_chip + 2 :]
    half = mine_ref.shape[0]
    parts = []
    for s in range(n_chip):
        parts += [arrived[s][:slots], swapped[half + s * slots : half + (s + 1) * slots]]
    touched = jnp.concatenate(parts, axis=0)
    negs = jnp.concatenate([stacked[:half], swapped[:half]], axis=0)
    trips = head_ref.shape[0]
    rows = take(both_picks(head_ref, tail_ref, slots, touched.shape[0]), touched)
    head, tail = rows[:trips], rows[trips:]
    query = join(hamilton(quarters(head), quarters(rot_ref[...])))
    positive = jnp.sum(query * tail, axis=-1, keepdims=True)
    pull_ref[...] = jnp.broadcast_to(-jax.nn.sigmoid(-positive), pull_ref.shape)
    query_ref[...], head_out[...], tail_out[...] = query, head, tail
    q_high, q_low = halves(query)
    n_high, n_low = halves(negs)
    scores = dot(
        jnp.concatenate([n_high, n_low, n_high], axis=1),
        jnp.concatenate([q_high, q_high, q_low], axis=1),
        COLS,
    )
    push = jax.nn.sigmoid(scores) * (1.0 / negs.shape[0])
    push_ref[...] = push
    p_high, p_low = halves(push)
    grad = dot(
        jnp.concatenate([p_high, p_low, p_high], axis=1),
        jnp.concatenate([q_high, q_high, q_low], axis=0),
        ROWS,
    )
    middle = mine_ref.shape[0]
    mine_ref[...] = grad[:middle]
    theirs_ref[...] = grad[middle:]


def grad_kernel(slots, half, head_ref, rel_index_ref, tail_ref, relation_ref, rot_ref, *refs):
    stacked, swapped, query_ref, head_rows, tail_rows, pull_ref, push_ref = refs[:7]
    rel_ref, touched_ref = refs[7:]
    negs = jnp.concatenate([stacked[:half], swapped[:half]], axis=0)
    p_high, p_low = halves(push_ref[...])
    n_high, n_low = halves(negs)
    pulled = dot(p_high, n_high, LEFT) + dot(p_low, n_high, LEFT) + dot(p_high, n_low, LEFT)
    pull = pull_ref[:, :1]
    grad_query = quarters(pulled + pull * tail_rows[...])
    grad_head = join(hamilton(grad_query, conjugate(quarters(rot_ref[...]))))
    grad_rot = join(hamilton(conjugate(quarters(head_rows[...])), grad_query))
    grad_tail = pull * query_ref[...]
    chosen = both_picks(head_ref, tail_ref, slots, touched_ref.shape[0])
    touched_ref[...] = put(chosen, jnp.concatenate([grad_head, grad_tail], axis=0))
    unit, inverse = unit_parts(relation_ref[...])
    chosen = pick(rel_index_ref[...].reshape(1, -1), relation_ref.shape[0])
    grad_unit = quarters(put(chosen, grad_rot))
    along = sum(u * g for u, g in zip(unit, grad_unit))
    rel_ref[...] = join([inverse * (g - u * along) for u, g in zip(unit, grad_unit)])


def select_kernel(part_ref, after_ref, *refs):
    blocks, out_ref = refs[: lax.axis_size("dom")], refs[-1]
    source = lax.axis_index("dom") ^ part_ref[0]
    picked = blocks[0][...]
    for s, ref in enumerate(blocks):
        picked = jnp.where(source == s, ref[...], picked)
    out_ref[...] = picked


def pack_kernel(slots, n_neg, mine, theirs, touched, rel, rel_ref, *back):
    rel_ref[...] = rel[...]
    for s, ref in enumerate(back):
        block = pl.ds(s * n_neg, n_neg)
        ref[: 2 * slots] = touched[2 * s * slots : 2 * (s + 1) * slots]
        ref[2 * slots :] = mine[block] + theirs[block]


def stack_kernel(order, neg_order, *refs):
    count = len(order)
    arrived, negs, out_ref = refs[:count], refs[count : 2 * count], refs[-1]
    n_neg, slots = negs[0].shape[0], arrived[0].shape[0] // 2
    for s, block in zip(neg_order, negs):
        out_ref[s * n_neg : (s + 1) * n_neg] = block[...]
    for s, rows in zip(order, arrived):
        start = count * n_neg + s * slots
        out_ref[start : start + slots] = rows[slots:]


def unpack_kernel(slots, order, *refs):
    back, (neg_ref, stay_ref, cross_ref) = refs[: len(order)], refs[-3:]
    neg_ref[...] = sum(ref[2 * slots :] for ref in back)
    for s, ref in zip(order, back):
        rows = pl.ds(s * slots, slots)
        stay_ref[rows] = ref[:slots]
        cross_ref[rows] = ref[slots : 2 * slots]


def adagrad(values, history, gradient):
    history_new = history + gradient * gradient
    return values - step_size * gradient * lax.rsqrt(history_new), history_new


def entity_kernel(part_ref, send_ref, neg_ref, entity_ref, acc_ref, stay_ref, cross_ref, *refs):
    negs, (out_ref, acc_out) = refs[:-2], refs[-2:]
    rel_here = lax.axis_index("rel")
    owner = (lax.axis_index("dom") == part_ref[0]).astype(jnp.float32)
    size = entity_ref.shape[0]
    slots = send_ref.shape[2]
    neg = sum(ref[...] for ref in negs) * owner
    chosen = [pick(neg_ref[pl.ds(rel_here, 1), :], size)]
    rows = [neg]
    for k, ref in ((0, stay_ref), (1, cross_ref)):
        for s in range(send_ref.shape[1] // 2):
            peer = (2 * s + k) ^ rel_here
            chosen.append(pick(send_ref[0, pl.ds(peer, 1), :], size))
            rows.append(ref[s * slots : (s + 1) * slots])
    grad = put(jnp.concatenate(chosen, axis=1), jnp.concatenate(rows, axis=0))
    out_ref[...], acc_out[...] = adagrad(entity_ref[...], acc_ref[...], grad)


def relation_kernel(*refs):
    *parts, relation_ref, acc_ref, out_ref, acc_out = refs
    grad = sum(ref[...] for ref in parts)
    out_ref[...], acc_out[...] = adagrad(relation_ref[...], acc_ref[...], grad)


def update_kernel(count, *refs):
    new_rel, (new_ent, ins) = refs[-2:], (refs[-4:-2], refs[:-4])
    relation_kernel(*ins[-2 - count :], *new_rel)
    entity_kernel(*ins[: -2 - count], *new_ent)


def shards(
    entity,
    entity_acc,
    relation,
    relation_acc,
    send_rows,
    trip_head,
    trip_rel,
    trip_tail,
    neg_part,
    neg_rows,
    *,
    n_dom,
    n_rel,
):
    ents, width = entity.shape
    rels = relation.shape[0]
    trips = trip_head.shape[0]
    slots = send_rows.shape[2]
    n_neg = neg_rows.shape[1]
    n_chip = n_rel // 2

    order = [*range(2, n_chip), *range(min(n_chip, 2))]
    own_negs, *parcels = call(
        gather_kernel,
        [(n_neg, width)] + [(2 * slots, width)] * n_chip,
        [HBM, HBM, HBM],
        (send_rows, neg_rows, entity),
        limit=60 * 1024,
        scratch=[
            pltpu.VMEM(entity.shape, jnp.float32),
            pltpu.SMEM(send_rows.shape, jnp.int32),
            pltpu.SMEM(neg_rows.shape, jnp.int32),
            pltpu.SemaphoreType.DMA((3,)),
        ],
    )
    spread = [own_negs] + [exchange(own_negs, "dom", n_dom, s) for s in range(1, n_dom)]
    arrived = [parcels[0]] + [exchange(parcels[s], "rel", n_rel, 2 * s) for s in range(1, n_chip)]
    (rot,) = call(rotation_kernel, [(trips, width)], [VMEM] * 2, (trip_rel, relation))
    (picked,) = call(
        select_kernel,
        [own_negs.shape],
        [SMEM, VMEM] + [VMEM] * (n_dom + len(arrived[1:2])),
        (neg_part, rot, *spread, *arrived[1:2]),
    )
    negs = [picked] + [exchange(picked, "rel", n_rel, 2 * s) for s in range(1, n_chip)]
    neg_order = [*range(2, n_chip)][::-1] + [*range(min(n_chip, 2))]
    (stacked,) = call(
        functools.partial(stack_kernel, order, neg_order),
        [(n_chip * (n_neg + slots), width)],
        [VMEM] * (2 * n_chip),
        (*[arrived[s] for s in order], *[negs[s] for s in neg_order]),
    )
    swapped = exchange(stacked, "rel", n_rel, 1)

    mine, theirs, *saved = call(
        functools.partial(scores_kernel, slots, n_chip),
        [(n_chip * n_neg, width)] * 2 + [(trips, width)] * 3 + [(trips, 128), (n_rel * n_neg, trips)],
        [VMEM] * (5 + n_chip),
        (trip_head, trip_tail, rot, *arrived, stacked, swapped),
    )
    theirs = exchange(theirs, "rel", n_rel, 1)
    rel_grad, touched = call(
        functools.partial(grad_kernel, slots, n_chip * n_neg),
        [relation.shape, (n_rel * slots, width)],
        [VMEM] * 12,
        (trip_head, trip_rel, trip_tail, relation, rot, stacked, swapped, *saved),
    )

    rel_grad, *back = call(
        functools.partial(pack_kernel, slots, n_neg),
        [relation.shape] + [(2 * slots + n_neg, width)] * n_chip,
        [VMEM] * 4,
        (mine, theirs, touched, rel_grad),
    )
    back = [back[0]] + [exchange(back[s], "rel", n_rel, 2 * s) for s in range(1, n_chip)]
    bits = [1 << b for b in range((n_dom - 1).bit_length())]
    sums = [rel_grad]
    for up, down in zip(bits, bits[::-1]):
        total = sum(sums)
        sums = [total, cross_exchange(total, n_dom, n_rel, up, down)]
    back_order = [*range(2, n_chip, 2), *range(min(n_chip, 2))[::-1], *range(3, n_chip, 2)]
    neg_share, stay, cross = call(
        functools.partial(unpack_kernel, slots, back_order),
        [(n_neg, width)] + [(n_chip * slots, width)] * 2,
        [VMEM] * n_chip,
        [back[s] for s in back_order],
    )
    neg_shares = [neg_share] + [exchange(neg_share, "dom", n_dom, s) for s in range(1, n_dom)]
    cross = exchange(cross, "rel", n_rel, 1)

    new_entity, new_entity_acc, new_relation, new_relation_acc = call(
        functools.partial(update_kernel, len(sums)),
        [entity.shape] * 2 + [relation.shape] * 2,
        [SMEM] + [VMEM] * (8 + n_dom + len(sums)),
        (neg_part, send_rows, neg_rows, entity, entity_acc, stay, cross)
        + (*neg_shares, *sums, relation, relation_acc),
    )
    return (new_entity, new_entity_acc, new_relation, new_relation_acc)


def solution(mesh):
    def step(*arrays):
        return shards(*arrays, n_dom=mesh.shape["dom"], n_rel=mesh.shape["rel"])

    both = ("dom", "rel")
    in_specs = (
        P(both, None),
        P(both, None),
        P("rel", None),
        P("rel", None),
        P(both, None, None),
        P(both),
        P(both),
        P(both),
        P(),
        P(),
    )
    out_specs = (P(both, None), P(both, None), P("rel", None), P("rel", None))
    return jax.shard_map(step, mesh=mesh, in_specs=in_specs, out_specs=out_specs, check_vma=False)
```

```python
import functools

import jax
import jax.numpy as jnp
from jax import lax
from jax.experimental import pallas as pl
from jax.experimental.pallas import tpu as pltpu
from jax.sharding import PartitionSpec as P

step_size = 0.05
SMEM = pl.BlockSpec(memory_space=pltpu.SMEM)
VMEM = pl.BlockSpec(memory_space=pltpu.VMEM)
HBM = pl.BlockSpec(memory_space=pltpu.HBM)
ROWS = ((1,), (0,))
COLS = ((1,), (1,))
LEFT = ((0,), (0,))


def exchange(block, axis, size, step):
    return lax.ppermute(block, axis, [(i, i ^ step) for i in range(size)])


def cross_exchange(block, n_dom, n_rel, even, odd):
    pairs = []
    for i in range(n_dom):
        for r in range(n_rel):
            pairs.append((i * n_rel + r, (i ^ (odd if r % 2 else even)) * n_rel + r))
    return lax.ppermute(block, ("dom", "rel"), pairs)


def other_way(step):
    return step ^ 3 if step % 4 in (1, 2) else step


def call(body, outs, specs, args, flops=0, scratch=(), limit=40 * 1024):
    shapes = [jax.ShapeDtypeStruct(shape, jnp.float32) for shape in outs]
    moved = 4 * sum(int(a.size) for a in args) + 4 * sum(int(s.size) for s in shapes)
    return pl.pallas_call(
        body,
        out_shape=shapes,
        in_specs=specs,
        out_specs=[VMEM] * len(shapes),
        scratch_shapes=scratch,
        compiler_params=pltpu.CompilerParams(vmem_limit_bytes=limit * 1024),
        cost_estimate=pl.CostEstimate(flops=flops, bytes_accessed=moved, transcendentals=0),
    )(*args)


def dot(left, right, dims):
    return lax.dot_general(left, right, (dims, ((), ())), preferred_element_type=jnp.float32)


def halves(rows):
    high = rows.astype(jnp.bfloat16)
    low = (rows - high.astype(jnp.float32)).astype(jnp.bfloat16)
    return high, low


def pick(index, size):
    spots = lax.broadcasted_iota(jnp.int32, (size, index.shape[1]), 0)
    return (spots == index).astype(jnp.float32)


def take(chosen, table):
    high, low = halves(table)
    chosen = chosen.astype(jnp.bfloat16)
    return dot(
        jnp.concatenate([chosen, chosen], axis=0), jnp.concatenate([high, low], axis=0), LEFT
    )


def put(chosen, rows):
    high, low = halves(rows)
    chosen = chosen.astype(jnp.bfloat16)
    return dot(chosen, high, ROWS) + dot(chosen, low, ROWS)


def quarters(rows):
    size = rows.shape[-1] // 4
    return [rows[:, i * size : (i + 1) * size] for i in range(4)]


def hamilton(left, right):
    la, lb, lc, ld = left
    ra, rb, rc, rd = right
    return [
        la * ra - lb * rb - lc * rc - ld * rd,
        la * rb + lb * ra + lc * rd - ld * rc,
        la * rc - lb * rd + lc * ra + ld * rb,
        la * rd + lb * rc - lc * rb + ld * ra,
    ]


def conjugate(parts):
    return [parts[0], -parts[1], -parts[2], -parts[3]]


def join(parts):
    return jnp.concatenate(parts, axis=-1)


def gather_kernel(send_ref, neg_ref, entity_ref, negs, *refs):
    *parcels, rows, sends, picks, sems = refs
    copies = [
        pltpu.make_async_copy(source, target, sems.at[i])
        for i, (source, target) in enumerate(
            ((entity_ref, rows), (send_ref, sends), (neg_ref, picks))
        )
    ]
    for copy in copies:
        copy.start()
    for copy in copies:
        copy.wait()
    rel_here = lax.axis_index("rel")
    slots = send_ref.shape[2]
    for i in range(neg_ref.shape[1]):
        negs[pl.ds(i, 1), :] = rows[pl.ds(picks[rel_here, i], 1), :]
    for s, ref in enumerate(parcels):
        for core in range(2):
            peer = (2 * s + core) ^ rel_here
            for t in range(slots):
                ref[pl.ds(core * slots + t, 1), :] = rows[pl.ds(sends[0, peer, t], 1), :]


def unit_parts(rows):
    parts = quarters(rows)
    inverse = lax.rsqrt(sum(part * part for part in parts))
    return [part * inverse for part in parts], inverse


def rotation_kernel(rel_index_ref, relation_ref, rot_ref):
    unit, _ = unit_parts(relation_ref[...])
    chosen = pick(rel_index_ref[...].reshape(1, -1), relation_ref.shape[0])
    rot_ref[...] = take(chosen, join(unit))


def relative(index_ref, rel_here, slots):
    index = index_ref[...].reshape(1, -1)
    return ((index // slots) ^ rel_here) * slots + index % slots


def both_picks(head_ref, tail_ref, slots, size):
    rel_here = lax.axis_index("rel")
    heads = pick(relative(head_ref, rel_here, slots), size)
    tails = pick(relative(tail_ref, rel_here, slots), size)
    return jnp.concatenate([heads, tails], axis=1)


def scores_kernel(
    slots, n_chip, head_ref, tail_ref, rot_ref, *refs
):
    arrived, (stacked, swapped) = refs[:n_chip], refs[n_chip : n_chip + 2]
    mine_ref, theirs_ref, query_ref, head_out, tail_out, pull_ref, push_ref = refs[n_chip + 2 :]
    half = mine_ref.shape[0]
    parts = []
    for s in range(n_chip):
        parts += [arrived[s][:slots], swapped[half + s * slots : half + (s + 1) * slots]]
    touched = jnp.concatenate(parts, axis=0)
    negs = jnp.concatenate([stacked[:half], swapped[:half]], axis=0)
    trips = head_ref.shape[0]
    rows = take(both_picks(head_ref, tail_ref, slots, touched.shape[0]), touched)
    head, tail = rows[:trips], rows[trips:]
    query = join(hamilton(quarters(head), quarters(rot_ref[...])))
    positive = jnp.sum(query * tail, axis=-1, keepdims=True)
    pull_ref[...] = jnp.broadcast_to(-jax.nn.sigmoid(-positive), pull_ref.shape)
    query_ref[...], head_out[...], tail_out[...] = query, head, tail
    q_high, q_low = halves(query)
    n_high, n_low = halves(negs)
    scores = dot(
        jnp.concatenate([n_high, n_low, n_high], axis=1),
        jnp.concatenate([q_high, q_high, q_low], axis=1),
        COLS,
    )
    push = jax.nn.sigmoid(scores) * (1.0 / negs.shape[0])
    push_ref[...] = push
    p_high, p_low = halves(push)
    grad = dot(
        jnp.concatenate([p_high, p_low, p_high], axis=1),
        jnp.concatenate([q_high, q_high, q_low], axis=0),
        ROWS,
    )
    middle = mine_ref.shape[0]
    mine_ref[...] = grad[:middle]
    theirs_ref[...] = grad[middle:]


def grad_kernel(slots, half, head_ref, rel_index_ref, tail_ref, relation_ref, rot_ref, *refs):
    stacked, swapped, query_ref, head_rows, tail_rows, pull_ref, push_ref = refs[:7]
    rel_ref, touched_ref = refs[7:]
    negs = jnp.concatenate([stacked[:half], swapped[:half]], axis=0)
    p_high, p_low = halves(push_ref[...])
    n_high, n_low = halves(negs)
    pulled = dot(p_high, n_high, LEFT) + dot(p_low, n_high, LEFT) + dot(p_high, n_low, LEFT)
    pull = pull_ref[:, :1]
    grad_query = quarters(pulled + pull * tail_rows[...])
    grad_head = join(hamilton(grad_query, conjugate(quarters(rot_ref[...]))))
    grad_rot = join(hamilton(conjugate(quarters(head_rows[...])), grad_query))
    grad_tail = pull * query_ref[...]
    chosen = both_picks(head_ref, tail_ref, slots, touched_ref.shape[0])
    touched_ref[...] = put(chosen, jnp.concatenate([grad_head, grad_tail], axis=0))
    unit, inverse = unit_parts(relation_ref[...])
    chosen = pick(rel_index_ref[...].reshape(1, -1), relation_ref.shape[0])
    grad_unit = quarters(put(chosen, grad_rot))
    along = sum(u * g for u, g in zip(unit, grad_unit))
    rel_ref[...] = join([inverse * (g - u * along) for u, g in zip(unit, grad_unit)])


def select_kernel(part_ref, *refs):
    blocks, out_ref = refs[: lax.axis_size("dom")], refs[-1]
    source = lax.axis_index("dom") ^ part_ref[0]
    picked = blocks[0][...]
    first_core = lax.axis_index("rel") % 2 == 0
    for s, ref in enumerate(blocks):
        step = jnp.where(first_core, s, other_way(s))
        picked = jnp.where(source == step, ref[...], picked)
    out_ref[...] = picked


def pack_kernel(slots, n_neg, mine, theirs, touched, rel, rel_ref, *back):
    rel_ref[...] = rel[...]
    for s, ref in enumerate(back):
        block = pl.ds(s * n_neg, n_neg)
        ref[: 2 * slots] = touched[2 * s * slots : 2 * (s + 1) * slots]
        ref[2 * slots :] = mine[block] + theirs[block]


def stack_kernel(order, neg_order, *refs):
    count = len(order)
    arrived, negs, out_ref = refs[:count], refs[count : 2 * count], refs[-1]
    n_neg, slots = negs[0].shape[0], arrived[0].shape[0] // 2
    for s, block in zip(neg_order, negs):
        out_ref[s * n_neg : (s + 1) * n_neg] = block[...]
    for s, rows in zip(order, arrived):
        start = count * n_neg + s * slots
        out_ref[start : start + slots] = rows[slots:]


def unpack_kernel(slots, order, *refs):
    back, (neg_ref, stay_ref, cross_ref) = refs[: len(order)], refs[-3:]
    neg_ref[...] = sum(ref[2 * slots :] for ref in back)
    for s, ref in zip(order, back):
        rows = pl.ds(s * slots, slots)
        stay_ref[rows] = ref[:slots]
        cross_ref[rows] = ref[slots : 2 * slots]


def adagrad(values, history, gradient):
    history_new = history + gradient * gradient
    return values - step_size * gradient * lax.rsqrt(history_new), history_new


def entity_kernel(part_ref, send_ref, neg_ref, entity_ref, acc_ref, stay_ref, cross_ref, *refs):
    negs, (out_ref, acc_out) = refs[:-2], refs[-2:]
    rel_here = lax.axis_index("rel")
    owner = (lax.axis_index("dom") == part_ref[0]).astype(jnp.float32)
    size = entity_ref.shape[0]
    slots = send_ref.shape[2]
    neg = sum(ref[...] for ref in negs) * owner
    chosen = [pick(neg_ref[pl.ds(rel_here, 1), :], size)]
    rows = [neg]
    for k, ref in ((0, stay_ref), (1, cross_ref)):
        for s in range(send_ref.shape[1] // 2):
            peer = (2 * s + k) ^ rel_here
            chosen.append(pick(send_ref[0, pl.ds(peer, 1), :], size))
            rows.append(ref[s * slots : (s + 1) * slots])
    grad = put(jnp.concatenate(chosen, axis=1), jnp.concatenate(rows, axis=0))
    out_ref[...], acc_out[...] = adagrad(entity_ref[...], acc_ref[...], grad)


def relation_kernel(*refs):
    *parts, relation_ref, acc_ref, out_ref, acc_out = refs
    grad = sum(ref[...] for ref in parts)
    out_ref[...], acc_out[...] = adagrad(relation_ref[...], acc_ref[...], grad)


def update_kernel(count, *refs):
    new_rel, (new_ent, ins) = refs[-2:], (refs[-4:-2], refs[:-4])
    relation_kernel(*ins[-2 - count :], *new_rel)
    entity_kernel(*ins[: -2 - count], *new_ent)


def shards(
    entity,
    entity_acc,
    relation,
    relation_acc,
    send_rows,
    trip_head,
    trip_rel,
    trip_tail,
    neg_part,
    neg_rows,
    *,
    n_dom,
    n_rel,
):
    ents, width = entity.shape
    rels = relation.shape[0]
    trips = trip_head.shape[0]
    slots = send_rows.shape[2]
    n_neg = neg_rows.shape[1]
    n_chip = n_rel // 2

    order = [*range(2, n_chip), *range(min(n_chip, 2))]
    own_negs, *parcels = call(
        gather_kernel,
        [(n_neg, width)] + [(2 * slots, width)] * n_chip,
        [HBM, HBM, HBM],
        (send_rows, neg_rows, entity),
        limit=60 * 1024,
        scratch=[
            pltpu.VMEM(entity.shape, jnp.float32),
            pltpu.SMEM(send_rows.shape, jnp.int32),
            pltpu.SMEM(neg_rows.shape, jnp.int32),
            pltpu.SemaphoreType.DMA((3,)),
        ],
    )
    spread = [own_negs] + [
        cross_exchange(own_negs, n_dom, n_rel, s, other_way(s)) for s in range(1, n_dom)
    ]
    arrived = [parcels[0]] + [exchange(parcels[s], "rel", n_rel, 2 * s) for s in range(1, n_chip)]
    (rot,) = call(rotation_kernel, [(trips, width)], [VMEM] * 2, (trip_rel, relation))
    (picked,) = call(
        select_kernel,
        [own_negs.shape],
        [SMEM] + [VMEM] * (n_dom + len(arrived[1:2])),
        (neg_part, *spread, *arrived[1:2]),
    )
    negs = [picked] + [exchange(picked, "rel", n_rel, 2 * s) for s in range(1, n_chip)]
    neg_order = [*range(2, n_chip)][::-1] + [*range(min(n_chip, 2))]
    (stacked,) = call(
        functools.partial(stack_kernel, order, neg_order),
        [(n_chip * (n_neg + slots), width)],
        [VMEM] * (2 * n_chip + 1),
        (*[arrived[s] for s in order], *[negs[s] for s in neg_order], rot),
    )
    swapped = exchange(stacked, "rel", n_rel, 1)

    mine, theirs, *saved = call(
        functools.partial(scores_kernel, slots, n_chip),
        [(n_chip * n_neg, width)] * 2 + [(trips, width)] * 3 + [(trips, 128), (n_rel * n_neg, trips)],
        [VMEM] * (5 + n_chip),
        (trip_head, trip_tail, rot, *arrived, stacked, swapped),
    )
    theirs = exchange(theirs, "rel", n_rel, 1)
    rel_grad, touched = call(
        functools.partial(grad_kernel, slots, n_chip * n_neg),
        [relation.shape, (n_rel * slots, width)],
        [VMEM] * 12,
        (trip_head, trip_rel, trip_tail, relation, rot, stacked, swapped, *saved),
    )

    rel_grad, *back = call(
        functools.partial(pack_kernel, slots, n_neg),
        [relation.shape] + [(2 * slots + n_neg, width)] * n_chip,
        [VMEM] * 4,
        (mine, theirs, touched, rel_grad),
    )
    back = [back[0]] + [exchange(back[s], "rel", n_rel, 2 * s) for s in range(1, n_chip)]
    bits = [1 << b for b in range((n_dom - 1).bit_length())]
    sums = [rel_grad]
    for up, down in zip(bits, bits[::-1]):
        total = sum(sums)
        sums = [total, cross_exchange(total, n_dom, n_rel, up, down)]
    back_order = [*range(2, n_chip, 2), *range(min(n_chip, 2))[::-1], *range(3, n_chip, 2)]
    neg_share, stay, cross = call(
        functools.partial(unpack_kernel, slots, back_order),
        [(n_neg, width)] + [(n_chip * slots, width)] * 2,
        [VMEM] * n_chip,
        [back[s] for s in back_order],
    )
    neg_shares = [neg_share] + [
        cross_exchange(neg_share, n_dom, n_rel, s, other_way(s)) for s in range(n_dom - 1, 0, -1)
    ]
    cross = exchange(cross, "rel", n_rel, 1)

    new_entity, new_entity_acc, new_relation, new_relation_acc = call(
        functools.partial(update_kernel, len(sums)),
        [entity.shape] * 2 + [relation.shape] * 2,
        [SMEM] + [VMEM] * (8 + n_dom + len(sums)),
        (neg_part, send_rows, neg_rows, entity, entity_acc, stay, cross)
        + (*neg_shares, *sums, relation, relation_acc),
    )
    return (new_entity, new_entity_acc, new_relation, new_relation_acc)


def solution(mesh):
    def step(*arrays):
        return shards(*arrays, n_dom=mesh.shape["dom"], n_rel=mesh.shape["rel"])

    both = ("dom", "rel")
    in_specs = (
        P(both, None),
        P(both, None),
        P("rel", None),
        P("rel", None),
        P(both, None, None),
        P(both),
        P(both),
        P(both),
        P(),
        P(),
    )
    out_specs = (P(both, None), P(both, None), P("rel", None), P("rel", None))
    return jax.shard_map(step, mesh=mesh, in_specs=in_specs, out_specs=out_specs, check_vma=False)
```

```python
import functools

import jax
import jax.numpy as jnp
from jax import lax
from jax.experimental import pallas as pl
from jax.experimental.pallas import tpu as pltpu
from jax.sharding import PartitionSpec as P

step_size = 0.05
SMEM = pl.BlockSpec(memory_space=pltpu.SMEM)
VMEM = pl.BlockSpec(memory_space=pltpu.VMEM)
HBM = pl.BlockSpec(memory_space=pltpu.HBM)
ROWS = ((1,), (0,))
COLS = ((1,), (1,))
LEFT = ((0,), (0,))


def exchange(block, axis, size, step):
    return lax.ppermute(block, axis, [(i, i ^ step) for i in range(size)])


def cross_exchange(block, n_dom, n_rel, even, odd):
    pairs = []
    for i in range(n_dom):
        for r in range(n_rel):
            pairs.append((i * n_rel + r, (i ^ (odd if r % 2 else even)) * n_rel + r))
    return lax.ppermute(block, ("dom", "rel"), pairs)


def call(body, outs, specs, args, flops=0, scratch=(), limit=40 * 1024):
    shapes = [jax.ShapeDtypeStruct(shape, jnp.float32) for shape in outs]
    moved = 4 * sum(int(a.size) for a in args) + 4 * sum(int(s.size) for s in shapes)
    return pl.pallas_call(
        body,
        out_shape=shapes,
        in_specs=specs,
        out_specs=[VMEM] * len(shapes),
        scratch_shapes=scratch,
        compiler_params=pltpu.CompilerParams(vmem_limit_bytes=limit * 1024),
        cost_estimate=pl.CostEstimate(flops=flops, bytes_accessed=moved, transcendentals=0),
    )(*args)


def dot(left, right, dims):
    return lax.dot_general(left, right, (dims, ((), ())), preferred_element_type=jnp.float32)


def halves(rows):
    high = rows.astype(jnp.bfloat16)
    low = (rows - high.astype(jnp.float32)).astype(jnp.bfloat16)
    return high, low


def pick(index, size):
    spots = lax.broadcasted_iota(jnp.int32, (size, index.shape[1]), 0)
    return (spots == index).astype(jnp.float32)


def take(chosen, table):
    high, low = halves(table)
    chosen = chosen.astype(jnp.bfloat16)
    return dot(
        jnp.concatenate([chosen, chosen], axis=0), jnp.concatenate([high, low], axis=0), LEFT
    )


def put(chosen, rows):
    high, low = halves(rows)
    chosen = chosen.astype(jnp.bfloat16)
    return dot(chosen, high, ROWS) + dot(chosen, low, ROWS)


def quarters(rows):
    size = rows.shape[-1] // 4
    return [rows[:, i * size : (i + 1) * size] for i in range(4)]


def hamilton(left, right):
    la, lb, lc, ld = left
    ra, rb, rc, rd = right
    return [
        la * ra - lb * rb - lc * rc - ld * rd,
        la * rb + lb * ra + lc * rd - ld * rc,
        la * rc - lb * rd + lc * ra + ld * rb,
        la * rd + lb * rc - lc * rb + ld * ra,
    ]


def conjugate(parts):
    return [parts[0], -parts[1], -parts[2], -parts[3]]


def join(parts):
    return jnp.concatenate(parts, axis=-1)


def gather_kernel(lists_ref, entity_ref, negs, *refs):
    *parcels, rows, lists, sems = refs
    copies = [
        pltpu.make_async_copy(source, target, sems.at[i])
        for i, (source, target) in enumerate(
            ((entity_ref, rows), (lists_ref, lists))
        )
    ]
    for copy in copies:
        copy.start()
    for copy in copies:
        copy.wait()
    rel_here = lax.axis_index("rel")
    n_rel, slots = 2 * len(parcels), parcels[0].shape[0] // 2
    for i in range(negs.shape[0]):
        negs[pl.ds(i, 1), :] = rows[pl.ds(lists[n_rel + rel_here, i], 1), :]
    for s, ref in enumerate(parcels):
        for core in range(2):
            peer = (2 * s + core) ^ rel_here
            for t in range(slots):
                ref[pl.ds(core * slots + t, 1), :] = rows[pl.ds(lists[peer, t], 1), :]


def unit_parts(rows):
    parts = quarters(rows)
    inverse = lax.rsqrt(sum(part * part for part in parts))
    return [part * inverse for part in parts], inverse


def rotation_kernel(rel_index_ref, relation_ref, rot_ref):
    unit, _ = unit_parts(relation_ref[...])
    chosen = pick(rel_index_ref[...].reshape(1, -1), relation_ref.shape[0])
    rot_ref[...] = take(chosen, join(unit))


def relative(index_ref, rel_here, slots):
    index = index_ref[...].reshape(1, -1)
    return ((index // slots) ^ rel_here) * slots + index % slots


def both_picks(head_ref, tail_ref, slots, size):
    rel_here = lax.axis_index("rel")
    heads = pick(relative(head_ref, rel_here, slots), size)
    tails = pick(relative(tail_ref, rel_here, slots), size)
    return jnp.concatenate([heads, tails], axis=1)


def scores_kernel(
    slots, n_chip, head_ref, tail_ref, rot_ref, *refs
):
    arrived, (stacked, swapped) = refs[:n_chip], refs[n_chip : n_chip + 2]
    mine_ref, theirs_ref, query_ref, head_out, tail_out, pull_ref, push_ref = refs[n_chip + 2 :]
    half = mine_ref.shape[0]
    parts = []
    for s in range(n_chip):
        parts += [arrived[s][:slots], swapped[half + s * slots : half + (s + 1) * slots]]
    touched = jnp.concatenate(parts, axis=0)
    negs = jnp.concatenate([stacked[:half], swapped[:half]], axis=0)
    trips = head_ref.shape[0]
    rows = take(both_picks(head_ref, tail_ref, slots, touched.shape[0]), touched)
    head, tail = rows[:trips], rows[trips:]
    query = join(hamilton(quarters(head), quarters(rot_ref[...])))
    positive = jnp.sum(query * tail, axis=-1, keepdims=True)
    pull_ref[...] = jnp.broadcast_to(-jax.nn.sigmoid(-positive), pull_ref.shape)
    query_ref[...], head_out[...], tail_out[...] = query, head, tail
    q_high, q_low = halves(query)
    n_high, n_low = halves(negs)
    scores = dot(
        jnp.concatenate([n_high, n_low, n_high], axis=1),
        jnp.concatenate([q_high, q_high, q_low], axis=1),
        COLS,
    )
    push = jax.nn.sigmoid(scores) * (1.0 / negs.shape[0])
    push_ref[...] = push
    p_high, p_low = halves(push)
    grad = dot(
        jnp.concatenate([p_high, p_low, p_high], axis=1),
        jnp.concatenate([q_high, q_high, q_low], axis=0),
        ROWS,
    )
    middle = mine_ref.shape[0]
    mine_ref[...] = grad[:middle]
    theirs_ref[...] = grad[middle:]


def grad_kernel(slots, half, head_ref, rel_index_ref, tail_ref, relation_ref, rot_ref, *refs):
    stacked, swapped, query_ref, head_rows, tail_rows, pull_ref, push_ref = refs[:7]
    rel_ref, touched_ref = refs[7:]
    negs = jnp.concatenate([stacked[:half], swapped[:half]], axis=0)
    p_high, p_low = halves(push_ref[...])
    n_high, n_low = halves(negs)
    pulled = dot(p_high, n_high, LEFT) + dot(p_low, n_high, LEFT) + dot(p_high, n_low, LEFT)
    pull = pull_ref[:, :1]
    grad_query = quarters(pulled + pull * tail_rows[...])
    grad_head = join(hamilton(grad_query, conjugate(quarters(rot_ref[...]))))
    grad_rot = join(hamilton(conjugate(quarters(head_rows[...])), grad_query))
    grad_tail = pull * query_ref[...]
    chosen = both_picks(head_ref, tail_ref, slots, touched_ref.shape[0])
    touched_ref[...] = put(chosen, jnp.concatenate([grad_head, grad_tail], axis=0))
    unit, inverse = unit_parts(relation_ref[...])
    chosen = pick(rel_index_ref[...].reshape(1, -1), relation_ref.shape[0])
    grad_unit = quarters(put(chosen, grad_rot))
    along = sum(u * g for u, g in zip(unit, grad_unit))
    rel_ref[...] = join([inverse * (g - u * along) for u, g in zip(unit, grad_unit)])


def select_kernel(part_ref, after_ref, *refs):
    blocks, out_ref = refs[: lax.axis_size("dom")], refs[-1]
    source = lax.axis_index("dom") ^ part_ref[0]
    picked = blocks[0][...]
    for s, ref in enumerate(blocks):
        picked = jnp.where(source == s, ref[...], picked)
    out_ref[...] = picked


def pack_kernel(slots, n_neg, mine, theirs, touched, rel, rel_ref, *back):
    rel_ref[...] = rel[...]
    for s, ref in enumerate(back):
        block = pl.ds(s * n_neg, n_neg)
        ref[: 2 * slots] = touched[2 * s * slots : 2 * (s + 1) * slots]
        ref[2 * slots :] = mine[block] + theirs[block]


def stack_kernel(order, neg_order, *refs):
    count = len(order)
    arrived, negs, out_ref = refs[:count], refs[count : 2 * count], refs[-1]
    n_neg, slots = negs[0].shape[0], arrived[0].shape[0] // 2
    for s, block in zip(neg_order, negs):
        out_ref[s * n_neg : (s + 1) * n_neg] = block[...]
    for s, rows in zip(order, arrived):
        start = count * n_neg + s * slots
        out_ref[start : start + slots] = rows[slots:]


def unpack_kernel(slots, order, *refs):
    back, (neg_ref, stay_ref, cross_ref) = refs[: len(order)], refs[-3:]
    neg_ref[...] = sum(ref[2 * slots :] for ref in back)
    for s, ref in zip(order, back):
        rows = pl.ds(s * slots, slots)
        stay_ref[rows] = ref[:slots]
        cross_ref[rows] = ref[slots : 2 * slots]


def adagrad(values, history, gradient):
    history_new = history + gradient * gradient
    return values - step_size * gradient * lax.rsqrt(history_new), history_new


def entity_kernel(part_ref, send_ref, neg_ref, entity_ref, acc_ref, stay_ref, cross_ref, *refs):
    negs, (out_ref, acc_out) = refs[:-2], refs[-2:]
    rel_here = lax.axis_index("rel")
    owner = (lax.axis_index("dom") == part_ref[0]).astype(jnp.float32)
    size = entity_ref.shape[0]
    slots = send_ref.shape[2]
    neg = sum(ref[...] for ref in negs) * owner
    chosen = [pick(neg_ref[pl.ds(rel_here, 1), :], size)]
    rows = [neg]
    for k, ref in ((0, stay_ref), (1, cross_ref)):
        for s in range(send_ref.shape[1] // 2):
            peer = (2 * s + k) ^ rel_here
            chosen.append(pick(send_ref[0, pl.ds(peer, 1), :], size))
            rows.append(ref[s * slots : (s + 1) * slots])
    grad = put(jnp.concatenate(chosen, axis=1), jnp.concatenate(rows, axis=0))
    out_ref[...], acc_out[...] = adagrad(entity_ref[...], acc_ref[...], grad)


def relation_kernel(*refs):
    *parts, relation_ref, acc_ref, out_ref, acc_out = refs
    grad = sum(ref[...] for ref in parts)
    out_ref[...], acc_out[...] = adagrad(relation_ref[...], acc_ref[...], grad)


def update_kernel(count, *refs):
    new_rel, (new_ent, ins) = refs[-2:], (refs[-4:-2], refs[:-4])
    relation_kernel(*ins[-2 - count :], *new_rel)
    entity_kernel(*ins[: -2 - count], *new_ent)


def shards(
    entity,
    entity_acc,
    relation,
    relation_acc,
    send_rows,
    trip_head,
    trip_rel,
    trip_tail,
    neg_part,
    neg_rows,
    *,
    n_dom,
    n_rel,
):
    ents, width = entity.shape
    rels = relation.shape[0]
    trips = trip_head.shape[0]
    slots = send_rows.shape[2]
    n_neg = neg_rows.shape[1]
    n_chip = n_rel // 2

    order = [*range(2, n_chip), *range(min(n_chip, 2))]
    wide = max(slots, n_neg)
    lists = jnp.concatenate(
        [
            jnp.pad(send_rows[0], ((0, 0), (0, wide - slots))),
            jnp.pad(neg_rows, ((0, 0), (0, wide - n_neg))),
        ]
    )
    own_negs, *parcels = call(
        gather_kernel,
        [(n_neg, width)] + [(2 * slots, width)] * n_chip,
        [HBM, HBM],
        (lists, entity),
        limit=54784,
        scratch=[
            pltpu.VMEM(entity.shape, jnp.float32),
            pltpu.SMEM(lists.shape, jnp.int32),
            pltpu.SemaphoreType.DMA((2,)),
        ],
    )
    spread = [own_negs] + [exchange(own_negs, "dom", n_dom, s) for s in range(1, n_dom)]
    arrived = [parcels[0]] + [exchange(parcels[s], "rel", n_rel, 2 * s) for s in range(1, n_chip)]
    (rot,) = call(rotation_kernel, [(trips, width)], [VMEM] * 2, (trip_rel, relation))
    (picked,) = call(
        select_kernel,
        [own_negs.shape],
        [SMEM, VMEM] + [VMEM] * (n_dom + len(arrived[1:2])),
        (neg_part, rot, *spread, *arrived[1:2]),
    )
    negs = [picked] + [exchange(picked, "rel", n_rel, 2 * s) for s in range(1, n_chip)]
    neg_order = [*range(2, n_chip)][::-1] + [*range(min(n_chip, 2))]
    (stacked,) = call(
        functools.partial(stack_kernel, order, neg_order),
        [(n_chip * (n_neg + slots), width)],
        [VMEM] * (2 * n_chip),
        (*[arrived[s] for s in order], *[negs[s] for s in neg_order]),
    )
    swapped = exchange(stacked, "rel", n_rel, 1)

    mine, theirs, *saved = call(
        functools.partial(scores_kernel, slots, n_chip),
        [(n_chip * n_neg, width)] * 2 + [(trips, width)] * 3 + [(trips, 128), (n_rel * n_neg, trips)],
        [VMEM] * (5 + n_chip),
        (trip_head, trip_tail, rot, *arrived, stacked, swapped),
    )
    theirs = exchange(theirs, "rel", n_rel, 1)
    rel_grad, touched = call(
        functools.partial(grad_kernel, slots, n_chip * n_neg),
        [relation.shape, (n_rel * slots, width)],
        [VMEM] * 12,
        (trip_head, trip_rel, trip_tail, relation, rot, stacked, swapped, *saved),
    )

    rel_grad, *back = call(
        functools.partial(pack_kernel, slots, n_neg),
        [relation.shape] + [(2 * slots + n_neg, width)] * n_chip,
        [VMEM] * 4,
        (mine, theirs, touched, rel_grad),
    )
    back = [back[0]] + [exchange(back[s], "rel", n_rel, 2 * s) for s in range(1, n_chip)]
    bits = [1 << b for b in range((n_dom - 1).bit_length())]
    sums = [rel_grad]
    for up, down in zip(bits, bits[::-1]):
        total = sum(sums)
        sums = [total, cross_exchange(total, n_dom, n_rel, up, down)]
    back_order = [*range(2, n_chip, 2), *range(min(n_chip, 2))[::-1], *range(3, n_chip, 2)]
    neg_share, stay, cross = call(
        functools.partial(unpack_kernel, slots, back_order),
        [(n_neg, width)] + [(n_chip * slots, width)] * 2,
        [VMEM] * n_chip,
        [back[s] for s in back_order],
    )
    neg_shares = [neg_share] + [exchange(neg_share, "dom", n_dom, s) for s in range(1, n_dom)]
    cross = exchange(cross, "rel", n_rel, 1)

    new_entity, new_entity_acc, new_relation, new_relation_acc = call(
        functools.partial(update_kernel, len(sums)),
        [entity.shape] * 2 + [relation.shape] * 2,
        [SMEM] + [VMEM] * (8 + n_dom + len(sums)),
        (neg_part, send_rows, neg_rows, entity, entity_acc, stay, cross)
        + (*neg_shares, *sums, relation, relation_acc),
    )
    return (new_entity, new_entity_acc, new_relation, new_relation_acc)


def solution(mesh):
    def step(*arrays):
        return shards(*arrays, n_dom=mesh.shape["dom"], n_rel=mesh.shape["rel"])

    both = ("dom", "rel")
    in_specs = (
        P(both, None),
        P(both, None),
        P("rel", None),
        P("rel", None),
        P(both, None, None),
        P(both),
        P(both),
        P(both),
        P(),
        P(),
    )
    out_specs = (P(both, None), P(both, None), P("rel", None), P("rel", None))
    return jax.shard_map(step, mesh=mesh, in_specs=in_specs, out_specs=out_specs, check_vma=False)
```
